512 devices in a mesh: lat: 16 (over x_lo, y, core), lon: 32 (over z, x_hi).
Axes of the slice: x: 4 (x_hi: 2, x_lo: 2; x = x_hi * 2 + x_lo), y: 4, z: 16, core: 2. Of those that a mesh axis runs over, the one named last changes fastest.
Arguments:
- tokens: bfloat16 [4, 192, 768, 512], P(None, 'lat', 'lon'), may hold values from -20 to 20
- region: int32 [4, 192, 768], P(None, 'lat', 'lon'), may hold values from 0 to 7
- qkv_weight: bfloat16 [512, 1536], P('lat', 'lon'), may hold values from -1 to 1
- proj_weight: bfloat16 [512, 512], P('lat', 'lon'), may hold values from -1 to 1
Outputs:
- blended: bfloat16 [4, 192, 768, 512], P(None, 'lat', 'lon')
The draws below stay inside these ranges and needn't reach their ends.
All inputs are finite; a program needn't handle non-finite values.
Results may differ from the reference program's by a relative error of at most 0.0066.
Values may be sent and summed in bfloat16 or wider, within the bound.
A program may use at most 64 MiB of HBM per device.

```python
import jax
import jax.numpy as jnp
from jax import lax

D = 512
HEADS = 8
WLEV = 2
WLAT = 6
WLON = 12
LEVELS = 4
NLAT = 192
NLON = 768


def draw_tokens(key, part):
    key = jax.random.fold_in(key, 1)
    noise_key = jax.random.fold_in(key, 0)
    grid = jax.random.truncated_normal(noise_key, -4.0, 4.0, (LEVELS, NLAT, NLON, D), jnp.float32)
    return grid.astype(jnp.bfloat16)


def draw_qkv_weight(key, part):
    key = jax.random.fold_in(key, 2)
    base_key = jax.random.fold_in(key, 0)
    matrix = jax.random.truncated_normal(base_key, -4.0, 4.0, (D, 3 * D), jnp.float32) * D ** (-0.5)
    return matrix.astype(jnp.bfloat16)


def draw_region(key, part):
    key = jax.random.fold_in(key, 3)
    shape = (LEVELS, NLAT, NLON)
    level_idx = lax.broadcasted_iota(jnp.int32, shape, 0)
    lat_idx = lax.broadcasted_iota(jnp.int32, shape, 1)
    coin = jax.random.randint(key, shape, 0, 2)
    lat_band = (lat_idx >= NLAT - WLAT // 2).astype(jnp.int32)
    level_band = (level_idx >= LEVELS - WLEV // 2).astype(jnp.int32)
    return (4 * lat_band + 2 * level_band + coin).astype(jnp.int32)


def levels(rng, extent, cuts, smallest, top_value):
    level, own = 1.0, jax.random.fold_in(rng, 6)
    for position, parts in cuts:
        heights = jnp.exp(jax.random.uniform(jax.random.fold_in(own, position), (parts,), jnp.float32, smallest / len(cuts), top_value / len(cuts)))
        level = level * jnp.repeat(heights, extent[position] // parts).reshape([-1 if axis == position else 1 for axis in range(len(extent))])
    return level


def scatter_about(rng, shape, deviation, reach, pieces=(), kind=jnp.bfloat16):
    level = levels(rng, shape, pieces, -0.22, 0.18) if pieces else 1.0
    entries = jax.random.normal(rng, shape, jnp.float32) * deviation * level
    return jnp.minimum(jnp.maximum(entries, -reach), reach).astype(kind)


def setup_inputs(seed: int = 0) -> dict:
    splits = jax.random.split(jax.random.key(seed), 5)
    tokens = draw_tokens(jax.random.fold_in(splits[4], 71), 0)
    region = draw_region(jax.random.fold_in(splits[4], 71), 0)
    qkv_weight = draw_qkv_weight(jax.random.fold_in(splits[4], 71), 0)
    proj_weight = scatter_about(splits[3], (D, D), (D // 16) ** -0.5, 1.0, ((0, 16), (1, 32)))
    return {"tokens": tokens, "region": region, "qkv_weight": qkv_weight, "proj_weight": proj_weight}


epsilon = 1e-05

def layer_normed(grid):
    floated = grid.astype(jnp.float32)
    average = lax.optimization_barrier(jnp.mean(floated, axis=-1, keepdims=True))
    centred = floated - average
    spread = lax.optimization_barrier(jnp.mean(centred * centred, axis=-1, keepdims=True))
    return (centred * lax.rsqrt(spread + epsilon)).astype(jnp.bfloat16)

def to_windows(grid):
    level_n, lat_n, lon_n, channels = grid.shape
    shaped = grid.reshape(level_n // WLEV, WLEV, lat_n // WLAT, WLAT, lon_n // WLON, WLON, channels)
    return shaped.transpose(0, 2, 4, 1, 3, 5, 6).reshape(-1, WLEV * WLAT * WLON, channels)

def from_windows(groups, level_n, lat_n, lon_n):
    channels = groups.shape[-1]
    shaped = groups.reshape(level_n // WLEV, lat_n // WLAT, lon_n // WLON, WLEV, WLAT, WLON, channels)
    return shaped.transpose(0, 3, 1, 4, 2, 5, 6).reshape(level_n, lat_n, lon_n, channels)

def windowed(qkv_grid, labels):
    level_n, lat_n, lon_n, triple = qkv_grid.shape
    features = triple // 3
    grouped = to_windows(qkv_grid)
    tags = to_windows(labels[..., None])[..., 0]
    allowed = tags[:, :, None] == tags[:, None, :]
    window_n, span_n = (grouped.shape[0], grouped.shape[1])
    split_heads = grouped.reshape(window_n, span_n, 3, HEADS, features // HEADS).transpose(2, 3, 0, 1, 4)
    factor = (features // HEADS) ** (-0.5)

    def one_head(triplet):
        queries, key_rows, value_rows = triplet
        scores = jnp.einsum('wqd,wkd->wqk', queries.astype(jnp.float32), key_rows.astype(jnp.float32)) * factor
        scores = jnp.where(allowed, scores, -jnp.inf)
        highest = lax.optimization_barrier(jnp.max(scores, axis=-1, keepdims=True))
        raised = jnp.exp(scores - highest)
        chances = (raised / lax.optimization_barrier(jnp.sum(raised, axis=-1, keepdims=True))).astype(jnp.bfloat16)
        mixed_rows = jnp.einsum('wqk,wkd->wqd', chances.astype(jnp.float32), value_rows.astype(jnp.float32))
        return mixed_rows.astype(jnp.bfloat16)
    per_head = lax.map(one_head, (split_heads[0], split_heads[1], split_heads[2]))
    joined = per_head.transpose(1, 2, 0, 3).reshape(window_n, span_n, features)
    return from_windows(joined, level_n, lat_n, lon_n)

def reference(tokens, region, qkv_weight, proj_weight):
    shifted = jnp.roll(tokens, (-(WLEV // 2), -(WLAT // 2), -(WLON // 2)), axis=(0, 1, 2))
    blocks = NLAT // WLAT
    stacked = shifted.reshape(LEVELS, blocks, WLAT, NLON, D).transpose(1, 0, 2, 3, 4)
    labels = region.reshape(LEVELS, blocks, WLAT, NLON).transpose(1, 0, 2, 3)

    def one_block(paired):
        rows_in, labels_in = paired
        normed = layer_normed(rows_in).reshape(-1, D)
        qkv = jnp.dot(normed, qkv_weight, preferred_element_type=jnp.float32).astype(jnp.bfloat16)
        return windowed(qkv.reshape(LEVELS, WLAT, NLON, 3 * D), labels_in)
    attended = lax.map(one_block, (stacked, labels))
    attended = attended.transpose(1, 0, 2, 3, 4).reshape(LEVELS, NLAT, NLON, D)
    restored = jnp.roll(attended, (WLEV // 2, WLAT // 2, WLON // 2), axis=(0, 1, 2))
    restored_blocks = restored.reshape(LEVELS, blocks, WLAT, NLON, D).transpose(1, 0, 2, 3, 4)
    token_blocks = tokens.reshape(LEVELS, blocks, WLAT, NLON, D).transpose(1, 0, 2, 3, 4)

    def project(paired):
        restored_in, tokens_in = paired
        branch = jnp.dot(restored_in.reshape(-1, D), proj_weight, preferred_element_type=jnp.float32)
        summed = tokens_in.reshape(-1, D).astype(jnp.float32) + branch
        return summed.astype(jnp.bfloat16).reshape(tokens_in.shape)
    blended = lax.map(project, (restored_blocks, token_blocks))
    return blended.transpose(1, 0, 2, 3, 4).reshape(LEVELS, NLAT, NLON, D)
```

```python
import jax
import jax.numpy as jnp
import numpy as np
from jax import lax
from jax.experimental import pallas as pl
from jax.experimental.pallas import tpu as pltpu
from jax.sharding import PartitionSpec as P

MESH = pl.DeviceIdType.MESH
BF16 = jnp.bfloat16
F32 = jnp.float32

LEVELS, ROWS, COLS, D = 4, 12, 24, 512
HEADS = 8
LEVEL = ROWS * COLS
SPAN = 144
EPS = 1e-05
SCALE = float(np.log2(np.e) / 8.0)

RELATIVE = [0, 1, 2, 3, 4, -1, -2, -3, -4, 5, 6, 7, 8, -5, -6, -7]
PARTS = ((0, 9), (9, 7))


def positions(levels, rows, cols, pad=0):
    found = [(l, a, o) for l in levels for a in rows for o in cols]
    return found + [None] * pad


def one_hot(dest, source):
    where = {place: i for i, place in enumerate(source) if place is not None}
    matrix = np.zeros((len(dest), len(source)), np.float32)
    for i, place in enumerate(dest):
        if place in where:
            matrix[i, where[place]] = 1.0
    return matrix


BOTH = (0, 1)
OWN = positions(BOTH, range(ROWS), range(COLS))
W_PACK = positions(BOTH, range(3, 12), range(6), 4)
N_PACK = positions(BOTH, range(3), range(6, 24), 4)
C_PACK = positions(BOTH, range(3), range(6), 12)
E_SIDE = positions(BOTH, range(3, 12), range(24, 30), 4)
S_SIDE = positions(BOTH, range(12, 15), range(6, 24), 4)
C_SIDE = positions(BOTH, range(12, 15), range(24, 30), 12)
WINDOWS = [
    positions(BOTH, range(3 + 6 * i, 9 + 6 * i), range(6 + 12 * j, 18 + 12 * j))
    for i in (1, 0)
    for j in (1, 0)
]

PACKS = [one_hot(pack, OWN) for pack in (W_PACK, N_PACK, C_PACK)]
GATHERS = [one_hot(window, OWN) for window in WINDOWS]
SIDES = [
    [one_hot(WINDOWS[0], E_SIDE), one_hot(WINDOWS[0], S_SIDE), one_hot(WINDOWS[0], C_SIDE)],
    [None, one_hot(WINDOWS[1], S_SIDE), None],
    [one_hot(WINDOWS[2], E_SIDE), None, None],
    [None, None, None],
]


def lane_moves():
    moves = np.zeros((4, 128, 512), np.float32)
    for m in range(4):
        for q in range(4):
            for k in range(32):
                moves[m, q * 32 + k, q * 128 + m * 32 + k] = 1.0
    return moves


SLABS = {0: (208, 80), 1: (208, 80), 2: (64, 160), 3: (64, 160)}


def own_level(pair, part):
    return (2 * pair + part + 1) % LEVELS


def nn(a, b):
    return lax.dot_general(a, b, (((1,), (0,)), ((), ())), preferred_element_type=F32)


def nt(a, b):
    return lax.dot_general(a, b, (((1,), (1,)), ((), ())), preferred_element_type=F32)


def kernel(
    tokens, tile, tag_rows, tag_cols, packs, gathers, sides, moves, packs_t, gathers_t, sides_t,
    out,
    normed, windows, qkv, attended, restored, raw, whole_qkv, whole_proj,
    w_out, n_out, c_out, w_in, n_in, c_in, w_back, n_back, c_back, w_home, n_home, c_home,
    z_send, z_recv, p_send, p_recv, core_send, core_recv, halo_send, halo_recv, back_send, back_recv,
):
    lat = lax.axis_index("lat")
    lon = lax.axis_index("lon")
    core = lat % 2
    y = (lat // 2) % 4
    x = (lon % 2) * 2 + lat // 8
    z = lon // 2

    def at(xx, yy, zz, cc):
        return ((xx % 2) * 8 + yy * 2 + cc, zz * 2 + xx // 2)

    def along_z(step):
        return at(x, y, (z + step + 16) % 16, core)

    def in_plane(j):
        return at((x + j // 4) % 4, (y + j % 4) % 4, z, core)

    def beside(d_lat, d_lon):
        return ((lat + d_lat + 16) % 16, (lon + d_lon + 32) % 32)

    peer = at(x, y, z, 1 - core)
    near = [s for s in RELATIVE if 0 < abs(s) <= 4]
    partners = [along_z(s) for s in near]
    partners += [peer]
    partners += [beside(a, b) for a, b in ((0, 1), (0, -1), (1, 0), (-1, 0), (1, 1), (-1, -1))]
    barrier = pltpu.get_barrier_semaphore()
    for partner in partners:
        pl.semaphore_signal(barrier, 1, device_id=partner, device_id_type=MESH)

    @pl.loop(1, 16)
    def _(j):
        pl.semaphore_signal(barrier, 1, device_id=in_plane(j), device_id_type=MESH)

    raw[0, 0, 0] = tile[...]

    @pl.loop(0, 24)
    def _(i):
        rows = pl.ds(pl.multiple_of(i * 48, 48), 48)
        floated = tokens[rows, :].astype(F32)
        average = jnp.mean(floated, axis=-1, keepdims=True)
        centred = floated - average
        spread = jnp.mean(centred * centred, axis=-1, keepdims=True)
        normed[rows, :] = (centred * lax.rsqrt(spread + EPS)).astype(BF16)

    def slab(pair, part, start, size):
        return normed[pl.ds(own_level(pair, part) * LEVEL + start, size), :]

    for pair in range(2):
        for buf, first, size, start, height in (
            (w_out, 0, 112, 64, 224), (n_out, 112, 112, 0, 80), (c_out, 224, 48, 0, 80),
        ):
            total = 0.0
            for part in range(2):
                chosen = packs[pl.ds(first, size), pl.ds(part * LEVEL, LEVEL)][:, start:start + height]
                total += nn(chosen, slab(pair, part, start, height))
            buf[pl.ds(pair * size, size), :] = total.astype(BF16)

    pl.semaphore_wait(barrier, len(partners) + 15)

    def remote(src, dst, send, recv, target):
        return pltpu.make_async_remote_copy(src, dst, send, recv, device_id=target, device_id_type=MESH)

    first = []
    for n, s in enumerate(near):
        slot = RELATIVE.index(-s)
        copy = remote(raw.at[0, 0, 0], raw.at[0, 0, slot], z_send.at[n], z_recv.at[slot], along_z(s))
        copy.start()
        first.append(copy)
    halos = []
    for n, (src, dst, target) in enumerate((
        (w_out, w_in, beside(0, -1)), (c_out, c_in, beside(-1, -1)), (n_out, n_in, beside(-1, 0)),
    )):
        copy = remote(src, dst, halo_send.at[n], halo_recv.at[n], target)
        copy.start()
        halos.append(copy)
    for copy in first:
        copy.wait_recv()

    far = [
        remote(raw.at[0, 0, pl.ds(1, 4)], raw.at[0, 0, pl.ds(9, 4)], z_send.at[8], z_recv.at[9], along_z(-4)),
        remote(raw.at[0, 0, pl.ds(5, 3)], raw.at[0, 0, pl.ds(13, 3)], z_send.at[9], z_recv.at[10], along_z(4)),
    ]
    for copy in far:
        copy.start()

    def spread(part, j):
        span = pl.ds(*PARTS[part])
        back = ((4 - j // 4) % 4) * 4 + (4 - j % 4) % 4
        return remote(
            raw.at[0, 0, span], raw.at[0, back, span], p_send.at[part, j], p_recv.at[part, back], in_plane(j)
        )

    def arrival(part, j):
        span = pl.ds(*PARTS[part])
        return remote(
            raw.at[0, 0, span], raw.at[0, j, span], p_send.at[part, j], p_recv.at[part, j], in_plane(j)
        )

    def relay(part, j):
        span = pl.ds(*PARTS[part])
        return remote(
            raw.at[0, j, span], raw.at[1, j, span], core_send.at[part, j], core_recv.at[part, j], peer
        )

    def send_part(part):
        relay(part, 0).start()

        @pl.loop(1, 16)
        def _(j):
            spread(part, j).start()

    send_part(0)
    for copy in far:
        copy.wait_recv()
    send_part(1)
    for part in range(2):

        @pl.loop(1, 16)
        def _(j):
            arrival(part, j).wait_recv()
            relay(part, j).start()

    for copy in halos:
        copy.wait_recv()
    beginnings = (0, 112, 224)
    sizes = (112, 112, 48)
    for pair in range(2):
        for w in range(4):
            start, height = SLABS[w]
            total = 0.0
            for part in range(2):
                chosen = gathers[w, :, pl.ds(part * LEVEL, LEVEL)][:, start:start + height]
                total += nn(chosen, slab(pair, part, start, height))
            for k, arrived in enumerate((w_in, n_in, c_in)):
                if SIDES[w][k] is not None:
                    total += nn(
                        sides[w, :, pl.ds(k * 128, sizes[k])], arrived[pl.ds(pair * sizes[k], sizes[k]), :]
                    )
            windows[2 * w + pair] = total.astype(BF16)

    for part in range(2):

        @pl.loop(0, 16)
        def _(j):
            relay(part, j).wait_recv()

    for x_hi in range(2):
        for group in range(4):
            x_lo, y_hi = group // 2, group % 2
            total = 0.0
            for member in range(4):
                y_lo, cc = member // 2, member % 2
                j = ((x_hi * 2 + x_lo - x + 4) % 4) * 4 + (y_hi * 2 + y_lo - y + 4) % 4
                piece = raw[(cc + core) % 2, j].reshape(256, 128)
                total += nn(piece, moves[member])
            total = total.astype(BF16)
            lanes = pl.ds(group * 128, 128)
            for s in range(16):
                band = ((z + RELATIVE[s] + 16) % 16) * 2 + x_hi
                for q in range(4):
                    block = total[s * 16:(s + 1) * 16, q * 128:(q + 1) * 128]
                    if q < 3:
                        whole_qkv[pl.ds(pl.multiple_of(band * 48 + q * 16, 16), 16), lanes] = block
                    else:
                        whole_proj[pl.ds(pl.multiple_of(band * 16, 16), 16), lanes] = block

    @pl.loop(0, 6)
    def _(n):
        weights = whole_qkv[pl.ds(pl.multiple_of(n * 256, 256), 256), :]
        for w in range(8):
            qkv[n, w] = nt(windows[w], weights).astype(BF16)

    lower = lax.broadcasted_iota(jnp.int32, (SPAN, 128), 1) < 64
    ones = jnp.ones((SPAN, 128), BF16)

    def attend(w):
        bias = jnp.where(tag_cols[w] == tag_rows[w], 0.0, -1e30)
        bias = jnp.concatenate([bias, bias], axis=0)
        for t in range(4):
            lanes = slice((t % 2) * 128, (t % 2) * 128 + 128)
            query = qkv[t // 2, w, :, lanes]
            zero = jnp.zeros_like(query)
            both = jnp.concatenate([jnp.where(lower, query, zero), jnp.where(lower, zero, query)], axis=0)
            score = nt(both, qkv[2 + t // 2, w, :, lanes]) + bias
            raised = jnp.exp2((score - jnp.max(score, axis=-1, keepdims=True)) * SCALE).astype(BF16)
            mixed = nn(raised, jnp.concatenate([qkv[4 + t // 2, w, :, lanes], ones], axis=1))
            top = jnp.where(lower, mixed[:SPAN, :128], mixed[SPAN:, :128])
            bottom = jnp.where(lower, mixed[:SPAN, 128:], mixed[SPAN:, 128:])
            attended[w, :, pl.ds(t * 128, 128)] = (top / bottom).astype(BF16)

    def give_back(k, buf, sources, pair):
        total = 0.0
        for w in sources:
            total += nn(sides_t[w, pl.ds(k * 128, sizes[k]), :], attended[2 * w + pair])
        buf[pl.ds(pair * sizes[k], sizes[k]), :] = total.astype(BF16)

    returns = []

    def send_back(k, src, dst, target):
        copy = remote(src, dst, back_send.at[k], back_recv.at[k], target)
        copy.start()
        returns.append(copy)

    @pl.loop(0, 2)
    def _(w):
        attend(w)

    for pair in range(2):
        give_back(2, c_back, (0,), pair)
    send_back(2, c_back, c_home, beside(1, 1))

    @pl.loop(4, 6)
    def _(w):
        attend(w)

    for pair in range(2):
        give_back(0, w_back, (0, 2), pair)
    send_back(0, w_back, w_home, beside(0, 1))

    @pl.loop(2, 4)
    def _(w):
        attend(w)

    for pair in range(2):
        give_back(1, n_back, (0, 1), pair)
    send_back(1, n_back, n_home, beside(1, 0))

    @pl.loop(6, 8)
    def _(w):
        attend(w)

    for pair in range(2):
        for part in range(2):
            total = 0.0
            for w in range(4):
                total += nn(gathers_t[w, pl.ds(part * LEVEL, LEVEL), :], attended[2 * w + pair])
            restored[own_level(pair, part)] = total

    for copy in returns:
        copy.wait_recv()
    for pair in range(2):
        for part in range(2):
            level = own_level(pair, part)
            total = restored[level]
            for k, home in enumerate((w_home, n_home, c_home)):
                total += nn(
                    packs_t[pl.ds(part * LEVEL, LEVEL), pl.ds(k * 128, sizes[k])],
                    home[pl.ds(pair * sizes[k], sizes[k]), :],
                )
            branch = nt(total.astype(BF16), whole_proj[...])
            rows = pl.ds(level * LEVEL, LEVEL)
            out[rows, :] = (tokens[rows, :].astype(F32) + branch).astype(BF16)

    for copy in first + far + halos + returns:
        copy.wait_send()
    for part in range(2):
        relay(part, 0).wait_send()

        @pl.loop(1, 16)
        def _(j):
            spread(part, j).wait_send()
            relay(part, j).wait_send()


def constants():
    packs = np.concatenate(PACKS, axis=0)
    gathers = np.stack(GATHERS)
    sides = np.zeros((3, SPAN, 384), np.float32)
    for w in range(3):
        for k, matrix in enumerate(SIDES[w]):
            if matrix is not None:
                sides[w, :, k * 128:k * 128 + matrix.shape[1]] = matrix
    packs_t = np.zeros((2 * LEVEL, 384), np.float32)
    for k, matrix in enumerate(PACKS):
        packs_t[:, k * 128:k * 128 + matrix.shape[0]] = matrix.T
    return [
        jnp.asarray(a, BF16)
        for a in (packs, gathers, sides, lane_moves(), packs_t, gathers.transpose(0, 2, 1), sides.transpose(0, 2, 1))
    ]


def local(tokens, region, qkv_weight, proj_weight):
    tile = jnp.concatenate([qkv_weight, proj_weight], axis=1).T
    tile = tile.reshape(4, 16, 32).transpose(1, 0, 2).reshape(16, 128)
    tags = region.reshape(2, 2, 2, 6, 2, 12).transpose(2, 4, 0, 1, 3, 5)[::-1, ::-1].reshape(8, SPAN)
    vmem = pl.BlockSpec(memory_space=pltpu.VMEM)
    dma = pltpu.SemaphoreType.DMA

    def pieces(dtype=BF16):
        return [pltpu.VMEM((n, D), dtype) for n in (224, 224, 96)]

    blended = pl.pallas_call(
        kernel,
        out_shape=jax.ShapeDtypeStruct((LEVELS * LEVEL, D), BF16),
        in_specs=[vmem] * 11,
        out_specs=vmem,
        scratch_shapes=[
            pltpu.VMEM((LEVELS * LEVEL, D), BF16),
            pltpu.VMEM((8, SPAN, D), BF16),
            pltpu.VMEM((6, 8, SPAN, 256), BF16),
            pltpu.VMEM((8, SPAN, D), BF16),
            pltpu.VMEM((LEVELS, LEVEL, D), F32),
            pltpu.VMEM((2, 16, 16, 16, 128), BF16),
            pltpu.VMEM((3 * D, D), BF16),
            pltpu.VMEM((D, D), BF16),
            *pieces(), *pieces(), *pieces(), *pieces(),
            dma((10,)), dma((11,)), dma((2, 16)), dma((2, 16)), dma((2, 16)), dma((2, 16)),
            dma((3,)), dma((3,)), dma((3,)), dma((3,)),
        ],
        compiler_params=pltpu.CompilerParams(
            collective_id=0, has_side_effects=True, vmem_limit_bytes=56 * 1024 * 1024
        ),
        name="attention_block",
    )(
        tokens.reshape(-1, D), tile, tags[:, None, :], tags[:, :, None], *constants()
    )
    return blended.reshape(tokens.shape)


def solution(mesh):
    placed = (P(None, "lat", "lon", None), P(None, "lat", "lon"), P("lat", "lon"), P("lat", "lon"))
    return jax.shard_map(
        local, mesh=mesh, in_specs=placed, out_specs=P(None, "lat", "lon", None), check_vma=False
    )
```

```python
import jax
import jax.numpy as jnp
import numpy as np
from jax import lax
from jax.experimental import pallas as pl
from jax.experimental.pallas import tpu as pltpu
from jax.sharding import PartitionSpec as P

MESH = pl.DeviceIdType.MESH
BF16 = jnp.bfloat16
F32 = jnp.float32

LEVELS, ROWS, COLS, D = 4, 12, 24, 512
HEADS = 8
LEVEL = ROWS * COLS
SPAN = 144
EPS = 1e-05
SCALE = float(np.log2(np.e) / 8.0)

RELATIVE = [0, 1, 2, 3, 4, -1, -2, -3, -4, 5, 6, 7, 8, -5, -6, -7]
PARTS = ((0, 9), (9, 7))


def positions(levels, rows, cols, pad=0):
    found = [(l, a, o) for l in levels for a in rows for o in cols]
    return found + [None] * pad


def one_hot(dest, source):
    where = {place: i for i, place in enumerate(source) if place is not None}
    matrix = np.zeros((len(dest), len(source)), np.float32)
    for i, place in enumerate(dest):
        if place in where:
            matrix[i, where[place]] = 1.0
    return matrix


BOTH = (0, 1)
OWN = positions(BOTH, range(ROWS), range(COLS))
W_PACK = positions(BOTH, range(3, 12), range(6), 4)
N_PACK = positions(BOTH, range(3), range(6, 24), 4)
C_PACK = positions(BOTH, range(3), range(6), 12)
E_SIDE = positions(BOTH, range(3, 12), range(24, 30), 4)
S_SIDE = positions(BOTH, range(12, 15), range(6, 24), 4)
C_SIDE = positions(BOTH, range(12, 15), range(24, 30), 12)
WINDOWS = [
    positions(BOTH, range(3 + 6 * i, 9 + 6 * i), range(6 + 12 * j, 18 + 12 * j))
    for j in (1, 0)
    for i in (1, 0)
]

PACKS = [one_hot(pack, OWN) for pack in (W_PACK, N_PACK, C_PACK)]
GATHERS = [one_hot(window, OWN) for window in WINDOWS]
SIDES = [
    [one_hot(WINDOWS[0], E_SIDE), one_hot(WINDOWS[0], S_SIDE), one_hot(WINDOWS[0], C_SIDE)],
    [one_hot(WINDOWS[1], E_SIDE), None, None],
    [None, one_hot(WINDOWS[2], S_SIDE), None],
    [None, None, None],
]


def lane_moves():
    moves = np.zeros((4, 128, 512), np.float32)
    for m in range(4):
        for q in range(4):
            for k in range(32):
                moves[m, q * 32 + k, q * 128 + m * 32 + k] = 1.0
    return moves


def tag_picks():
    rows = np.zeros((2, 2, SPAN, 12), np.float32)
    cols = np.zeros((2, SPAN, 24), np.float32)
    for n, (part, a, o) in enumerate(positions(BOTH, range(6), range(12))):
        for half in range(2):
            rows[half, part, n, 6 * half + a] = 1.0
            cols[half, n, 12 * half + o] = 1.0
    return rows, cols


SLABS = {0: (208, 80), 1: (64, 160), 2: (208, 80), 3: (64, 160)}


def own_level(pair, part):
    return (2 * pair + part + 1) % LEVELS


def nn(a, b):
    return lax.dot_general(a, b, (((1,), (0,)), ((), ())), preferred_element_type=F32)


def tn(a, b):
    return lax.dot_general(a, b, (((0,), (0,)), ((), ())), preferred_element_type=F32)


def nt(a, b):
    return lax.dot_general(a, b, (((1,), (1,)), ((), ())), preferred_element_type=F32)


def kernel(
    tokens_in, region_in, qkv_in, proj_in, packs_in, gathers_in, sides_in, moves_in, packs_t_in, gathers_t_in,
    sides_t_in, pick_rows_in, pick_cols_in,
    restored_out, proj_out,
    tokens, region, qkv_part, proj_part, packs, gathers, sides, moves, packs_t, gathers_t, sides_t, pick_rows, pick_cols,
    tag_rows, tag_cols, normed, windows, qkv, attended, restored, given, raw, whole_qkv, whole_proj,
    w_out, n_out, c_out, w_in, n_in, c_in, w_back, n_back, c_back, w_home, n_home, c_home,
    in_sem, out_sem,
    z_send, z_recv, p_send, p_recv, core_send, core_recv, halo_send, halo_recv, back_send, back_recv,
):
    lat = lax.axis_index("lat")
    lon = lax.axis_index("lon")
    core = lat % 2
    y = (lat // 2) % 4
    x = (lon % 2) * 2 + lat // 8
    z = lon // 2

    def at(xx, yy, zz, cc):
        return ((xx % 2) * 8 + yy * 2 + cc, zz * 2 + xx // 2)

    def along_z(step):
        return at(x, y, (z + step + 16) % 16, core)

    def one_way(d):
        return at((x + d * (1 - core)) % 4, (y + d * core) % 4, z, core)

    def other_way(d):
        return at((x + d * core) % 4, (y + d * (1 - core)) % 4, z, core)

    def beside(d_lat, d_lon):
        return ((lat + d_lat + 16) % 16, (lon + d_lon + 32) % 32)

    peer = at(x, y, z, 1 - core)
    near = [s for s in RELATIVE if 0 < abs(s) <= 4]
    partners = [along_z(s) for s in near]
    partners += [one_way(d) for d in (1, 2, 3)] + [other_way(d) for d in (1, 2, 3)] + [peer]
    partners += [beside(a, b) for a, b in ((0, 1), (0, -1), (1, 0), (-1, 0), (1, 1), (-1, -1))]
    barrier = pltpu.get_barrier_semaphore()
    for partner in partners:
        pl.semaphore_signal(barrier, 1, device_id=partner, device_id_type=MESH)

    loads = [
        pltpu.make_async_copy(src, dst, in_sem.at[n])
        for n, (src, dst) in enumerate((
            (qkv_in, qkv_part), (proj_in, proj_part), (tokens_in, tokens), (packs_in, packs), (region_in, region),
            (pick_rows_in, pick_rows), (pick_cols_in, pick_cols), (gathers_in, gathers), (sides_in, sides),
            (moves_in, moves), (sides_t_in, sides_t), (gathers_t_in, gathers_t), (packs_t_in, packs_t),
        ))
    ]
    for load in loads:
        load.start()

    loads[0].wait()
    loads[1].wait()
    line = lax.broadcasted_iota(jnp.int32, (32, 128), 0)
    lane = lax.broadcasted_iota(jnp.int32, (32, 128), 1)
    total = 0.0
    for q in range(4):
        place = jnp.where(lane == line + 32 * q, 1.0, 0.0).astype(BF16)
        if q < 3:
            total += tn(qkv_part[...], place)[q * 16:(q + 1) * 16]
        else:
            total += tn(proj_part[...], place)
    raw[0, 0, 0, 0] = total.astype(BF16)

    loads[2].wait()

    @pl.loop(0, LEVELS)
    def _(i):
        rows = pl.ds(pl.multiple_of(i * LEVEL, LEVEL), LEVEL)
        floated = tokens[rows, :].astype(F32)
        average = jnp.mean(floated, axis=-1, keepdims=True)
        centred = floated - average
        spread = jnp.mean(centred * centred, axis=-1, keepdims=True)
        normed[rows, :] = (centred * lax.rsqrt(spread + EPS)).astype(BF16)

    def slab(pair, part, start, size):
        return normed[pl.ds(own_level(pair, part) * LEVEL + start, size), :]

    loads[3].wait()
    for pair in range(2):
        for buf, first, size, start, height in (
            (w_out, 0, 112, 64, 224), (n_out, 112, 112, 0, 80), (c_out, 224, 48, 0, 80),
        ):
            total = 0.0
            for part in range(2):
                chosen = packs[pl.ds(first, size), pl.ds(part * LEVEL, LEVEL)][:, start:start + height]
                total += nn(chosen, slab(pair, part, start, height))
            buf[pl.ds(pair * size, size), :] = total.astype(BF16)

    pl.semaphore_wait(barrier, len(partners))

    def remote(src, dst, send, recv, target):
        return pltpu.make_async_remote_copy(src, dst, send, recv, device_id=target, device_id_type=MESH)

    first = []
    for n, s in enumerate(near):
        slot = RELATIVE.index(-s)
        copy = remote(raw.at[0, 0, 0, 0], raw.at[0, 0, 0, slot], z_send.at[n], z_recv.at[slot], along_z(s))
        copy.start()
        first.append(copy)
    halos = []
    for n, (src, dst, target) in enumerate((
        (w_out, w_in, beside(0, -1)), (c_out, c_in, beside(-1, -1)), (n_out, n_in, beside(-1, 0)),
    )):
        copy = remote(src, dst, halo_send.at[n], halo_recv.at[n], target)
        copy.start()
        halos.append(copy)
    for copy in first:
        copy.wait_recv()

    far = [
        remote(raw.at[0, 0, 0, pl.ds(1, 4)], raw.at[0, 0, 0, pl.ds(9, 4)], z_send.at[8], z_recv.at[9], along_z(-4)),
        remote(raw.at[0, 0, 0, pl.ds(5, 3)], raw.at[0, 0, 0, pl.ds(13, 3)], z_send.at[9], z_recv.at[10], along_z(4)),
    ]
    for copy in far:
        copy.start()

    def step_one(part, d):
        span = pl.ds(*PARTS[part])
        return remote(
            raw.at[0, 0, 0, span], raw.at[0, 4 - d, 0, span], p_send.at[part, d, 0], p_recv.at[part, 4 - d, 0], one_way(d)
        )

    def step_two(part, i, d):
        span = pl.ds(*PARTS[part])
        return remote(
            raw.at[0, i, 0, span], raw.at[0, i, 4 - d, span], p_send.at[part, i, d], p_recv.at[part, i, 4 - d], other_way(d)
        )

    def arrival(part, i, k):
        span = pl.ds(*PARTS[part])
        return remote(
            raw.at[0, 0, 0, span], raw.at[0, i, k, span], p_send.at[part, i, k], p_recv.at[part, i, k], peer
        )

    def relay(part, i, k):
        span = pl.ds(*PARTS[part])
        return remote(
            raw.at[0, i, k, span], raw.at[1, i, k, span], core_send.at[part, i, k], core_recv.at[part, i, k], peer
        )

    def begin(part):
        for d in (1, 3, 2):
            step_one(part, d).start()
        for d in (1, 3, 2):
            step_two(part, 0, d).start()
        relay(part, 0, 0).start()

    def forward(part):
        for i in (1, 3, 2):
            arrival(part, i, 0).wait_recv()
            for d in (1, 3, 2):
                step_two(part, i, d).start()
            relay(part, i, 0).start()

    begin(0)
    forward(0)
    for copy in far:
        copy.wait_recv()
    begin(1)
    forward(1)
    for part in range(2):

        @pl.loop(0, 4)
        def _(i):
            for k in (1, 3, 2):
                arrival(part, i, k).wait_recv()
                relay(part, i, k).start()

    for n in (4, 5, 6, 7, 8):
        loads[n].wait()
    for w in range(4):
        half_lat, half_lon = (1, 0, 1, 0)[w], (1, 1, 0, 0)[w]
        for pair in range(2):
            column = 0.0
            for part in range(2):
                ids = region[2 * pair + part].astype(F32).astype(BF16)
                column += nn(pick_rows[half_lat, part], ids)
            column = jnp.sum(column * pick_cols[half_lon].astype(F32), axis=-1, keepdims=True)
            square = (SPAN, SPAN)
            same = lax.broadcasted_iota(jnp.int32, square, 0) == lax.broadcasted_iota(jnp.int32, square, 1)
            spots = jnp.where(same, column, 0.0).astype(BF16)
            tag_cols[2 * w + pair] = column
            tag_rows[2 * w + pair] = nn(jnp.ones((8, SPAN), BF16), spots)

    for copy in halos:
        copy.wait_recv()
    beginnings = (0, 112, 224)
    sizes = (112, 112, 48)
    for pair in range(2):
        for w in range(4):
            start, height = SLABS[w]
            total = 0.0
            for part in range(2):
                chosen = gathers[w, :, pl.ds(part * LEVEL, LEVEL)][:, start:start + height]
                total += nn(chosen, slab(pair, part, start, height))
            for k, arrived in enumerate((w_in, n_in, c_in)):
                if SIDES[w][k] is not None:
                    total += nn(
                        sides[w, :, pl.ds(k * 128, sizes[k])], arrived[pl.ds(pair * sizes[k], sizes[k]), :]
                    )
            windows[pl.ds((2 * w + pair) * SPAN, SPAN), :] = total.astype(BF16)

    for part in range(2):

        @pl.loop(0, 4)
        def _(i):
            for k in range(4):
                relay(part, i, k).wait_recv()

    loads[9].wait()
    for x_hi in range(2):
        for group in range(4):
            x_lo, y_hi = group // 2, group % 2
            total = 0.0
            for member in range(4):
                y_lo, cc = member // 2, member % 2
                d_x, d_y = (x_hi * 2 + x_lo - x + 4) % 4, (y_hi * 2 + y_lo - y + 4) % 4
                i, k = (d_x, d_y) if cc == 0 else (d_y, d_x)
                piece = raw[(cc + core) % 2, i, k].reshape(256, 128)
                total += nn(piece, moves[member])
            total = total.astype(BF16)
            lanes = pl.ds(group * 128, 128)
            for s in range(16):
                band = ((z + RELATIVE[s] + 16) % 16) * 2 + x_hi
                for q in range(4):
                    block = total[s * 16:(s + 1) * 16, q * 128:(q + 1) * 128]
                    if q < 3:
                        whole_qkv[pl.ds(pl.multiple_of(band * 48 + q * 16, 16), 16), lanes] = block
                    else:
                        whole_proj[pl.ds(pl.multiple_of(band * 16, 16), 16), lanes] = block

    proj_copy = pltpu.make_async_copy(whole_proj, proj_out, out_sem.at[4])
    proj_copy.start()

    def project_in(half):
        rows = pl.ds(half * 4 * SPAN, 4 * SPAN)
        for n in range(6):
            qkv[n, rows, :] = nt(windows[rows, :], whole_qkv[pl.ds(n * 256, 256), :]).astype(BF16)

    lower = lax.broadcasted_iota(jnp.int32, (SPAN, 128), 1) < 64
    ones = jnp.ones((SPAN, 128), BF16)

    def attend(w):
        rows = pl.ds(pl.multiple_of(w * SPAN, 16), SPAN)
        bias = jnp.where(tag_cols[w] == tag_rows[w][0:1], 0.0, -1e30)
        bias = jnp.concatenate([bias, bias], axis=0)
        scores = []
        for t in range(4):
            lanes = slice((t % 2) * 128, (t % 2) * 128 + 128)
            query = qkv[t // 2, rows, lanes]
            zero = jnp.zeros_like(query)
            both = jnp.concatenate([jnp.where(lower, query, zero), jnp.where(lower, zero, query)], axis=0)
            scores.append(nt(both, qkv[2 + t // 2, rows, lanes]) + bias)
        raised = [
            jnp.exp2((score - jnp.max(score, axis=-1, keepdims=True)) * SCALE).astype(BF16) for score in scores
        ]
        for t in range(4):
            lanes = slice((t % 2) * 128, (t % 2) * 128 + 128)
            mixed = nn(raised[t], jnp.concatenate([qkv[4 + t // 2, rows, lanes], ones], axis=1))
            top = jnp.where(lower, mixed[:SPAN, :128], mixed[SPAN:, :128])
            bottom = jnp.where(lower, mixed[:SPAN, 128:], mixed[SPAN:, 128:])
            attended[w, :, pl.ds(t * 128, 128)] = (top / bottom).astype(BF16)

    def give_back(k, buf, sources, pair):
        total = 0.0
        for w in sources:
            total += nn(sides_t[w, pl.ds(k * 128, sizes[k]), :], attended[2 * w + pair])
        buf[pl.ds(pair * sizes[k], sizes[k]), :] = total.astype(BF16)

    returns = []

    def send_back(k, src, dst, target):
        copy = remote(src, dst, back_send.at[k], back_recv.at[k], target)
        copy.start()
        returns.append(copy)

    project_in(0)

    @pl.loop(0, 2)
    def _(w):
        attend(w)

    loads[10].wait()
    for pair in range(2):
        give_back(2, c_back, (0,), pair)
    send_back(2, c_back, c_home, beside(1, 1))

    @pl.loop(2, 4)
    def _(w):
        attend(w)

    for pair in range(2):
        give_back(0, w_back, (0, 1), pair)
    send_back(0, w_back, w_home, beside(0, 1))

    project_in(1)

    @pl.loop(4, 6)
    def _(w):
        attend(w)

    for pair in range(2):
        give_back(1, n_back, (0, 2), pair)
    send_back(1, n_back, n_home, beside(1, 0))

    @pl.loop(6, 8)
    def _(w):
        attend(w)

    loads[11].wait()
    for pair in range(2):
        for part in range(2):
            total = 0.0
            for w in range(4):
                total += nn(gathers_t[w, pl.ds(part * LEVEL, LEVEL), :], attended[2 * w + pair])
            restored[own_level(pair, part)] = total

    loads[12].wait()
    for copy in returns:
        copy.wait_recv()
    written = [proj_copy]
    for pair in range(2):
        for part in range(2):
            level = own_level(pair, part)
            total = restored[level]
            for k, home in enumerate((w_home, n_home, c_home)):
                total += nn(
                    packs_t[pl.ds(part * LEVEL, LEVEL), pl.ds(k * 128, sizes[k])],
                    home[pl.ds(pair * sizes[k], sizes[k]), :],
                )
            rows = pl.ds(level * LEVEL, LEVEL)
            given[rows, :] = total.astype(BF16)
            copy = pltpu.make_async_copy(given.at[rows, :], restored_out.at[rows, :], out_sem.at[level])
            copy.start()
            written.append(copy)

    for copy in first + far + halos + returns:
        copy.wait_send()
    for part in range(2):
        for d in (1, 2, 3):
            step_one(part, d).wait_send()

        @pl.loop(0, 4)
        def _(i):
            for d in (1, 2, 3):
                step_two(part, i, d).wait_send()
            for k in range(4):
                relay(part, i, k).wait_send()

    for copy in written:
        copy.wait()


def constants():
    packs = np.concatenate(PACKS, axis=0)
    gathers = np.stack(GATHERS)
    sides = np.zeros((3, SPAN, 384), np.float32)
    for w in range(3):
        for k, matrix in enumerate(SIDES[w]):
            if matrix is not None:
                sides[w, :, k * 128:k * 128 + matrix.shape[1]] = matrix
    packs_t = np.zeros((2 * LEVEL, 384), np.float32)
    for k, matrix in enumerate(PACKS):
        packs_t[:, k * 128:k * 128 + matrix.shape[0]] = matrix.T
    pick_rows, pick_cols = tag_picks()
    return [
        jnp.asarray(a, BF16)
        for a in (
            packs, gathers, sides, lane_moves(), packs_t, gathers.transpose(0, 2, 1), sides.transpose(0, 2, 1),
            pick_rows, pick_cols,
        )
    ]


def local(tokens, region, qkv_weight, proj_weight):
    flat = tokens.reshape(-1, D)
    operands = [flat, region, qkv_weight, proj_weight, *constants()]
    anywhere = pl.BlockSpec(memory_space=pl.ANY)
    dma = pltpu.SemaphoreType.DMA

    def pieces():
        return [pltpu.VMEM((n, D), BF16) for n in (224, 224, 96)]

    restored, whole_proj = pl.pallas_call(
        kernel,
        out_shape=[jax.ShapeDtypeStruct(flat.shape, BF16), jax.ShapeDtypeStruct((D, D), BF16)],
        in_specs=[anywhere] * len(operands),
        out_specs=[anywhere] * 2,
        scratch_shapes=[
            *[pltpu.VMEM(a.shape, a.dtype) for a in operands],
            pltpu.VMEM((8, 8, SPAN), F32),
            pltpu.VMEM((8, SPAN, 1), F32),
            pltpu.VMEM((LEVELS * LEVEL, D), BF16),
            pltpu.VMEM((8 * SPAN, D), BF16),
            pltpu.VMEM((6, 8 * SPAN, 256), BF16),
            pltpu.VMEM((8, SPAN, D), BF16),
            pltpu.VMEM((LEVELS, LEVEL, D), F32),
            pltpu.VMEM((LEVELS * LEVEL, D), BF16),
            pltpu.VMEM((2, 4, 4, 16, 16, 128), BF16),
            pltpu.VMEM((3 * D, D), BF16),
            pltpu.VMEM((D, D), BF16),
            *pieces(), *pieces(), *pieces(), *pieces(),
            dma((len(operands),)), dma((5,)),
            dma((10,)), dma((11,)), dma((2, 4, 4)), dma((2, 4, 4)), dma((2, 4, 4)), dma((2, 4, 4)),
            dma((3,)), dma((3,)), dma((3,)), dma((3,)),
        ],
        compiler_params=pltpu.CompilerParams(
            collective_id=0, has_side_effects=True, vmem_limit_bytes=56 * 1024 * 1024
        ),
        name="attention_block",
    )(*operands)
    blended = flat.astype(F32) + nt(restored, whole_proj)
    return blended.astype(BF16).reshape(tokens.shape)


def solution(mesh):
    placed = (P(None, "lat", "lon", None), P(None, "lat", "lon"), P("lat", "lon"), P("lat", "lon"))
    return jax.shard_map(
        local, mesh=mesh, in_specs=placed, out_specs=P(None, "lat", "lon", None), check_vma=False
    )
```

```python
import jax
import jax.numpy as jnp
import numpy as np
from jax import lax
from jax.experimental import pallas as pl
from jax.experimental.pallas import tpu as pltpu
from jax.sharding import PartitionSpec as P

MESH = pl.DeviceIdType.MESH
BF16 = jnp.bfloat16
F32 = jnp.float32

LEVELS, ROWS, COLS, D = 4, 12, 24, 512
HEADS = 8
LEVEL = ROWS * COLS
SPAN = 144
EPS = 1e-05
SCALE = float(np.log2(np.e) / 8.0)

RELATIVE = [0, 1, 2, 3, 4, -1, -2, -3, -4, 5, 6, 7, 8, -5, -6, -7]
PARTS = ((0, 9), (9, 7))


def positions(levels, rows, cols, pad=0):
    found = [(l, a, o) for l in levels for a in rows for o in cols]
    return found + [None] * pad


def one_hot(dest, source):
    where = {place: i for i, place in enumerate(source) if place is not None}
    matrix = np.zeros((len(dest), len(source)), np.float32)
    for i, place in enumerate(dest):
        if place in where:
            matrix[i, where[place]] = 1.0
    return matrix


BOTH = (0, 1)
OWN = positions(BOTH, range(ROWS), range(COLS))
W_PACK = positions(BOTH, range(3, 12), range(6), 4)
N_PACK = positions(BOTH, range(3), range(6, 24), 4)
C_PACK = positions(BOTH, range(3), range(6), 12)
E_SIDE = positions(BOTH, range(3, 12), range(24, 30), 4)
S_SIDE = positions(BOTH, range(12, 15), range(6, 24), 4)
C_SIDE = positions(BOTH, range(12, 15), range(24, 30), 12)
WINDOWS = [
    positions(BOTH, range(3 + 6 * i, 9 + 6 * i), range(6 + 12 * j, 18 + 12 * j))
    for j in (1, 0)
    for i in (1, 0)
]

PACKS = [one_hot(pack, OWN) for pack in (W_PACK, N_PACK, C_PACK)]
GATHERS = [one_hot(window, OWN) for window in WINDOWS]
SIDES = [
    [one_hot(WINDOWS[0], E_SIDE), one_hot(WINDOWS[0], S_SIDE), one_hot(WINDOWS[0], C_SIDE)],
    [one_hot(WINDOWS[1], E_SIDE), None, None],
    [None, one_hot(WINDOWS[2], S_SIDE), None],
    [None, None, None],
]


def lane_moves():
    moves = np.zeros((4, 128, 512), np.float32)
    for m in range(4):
        for q in range(4):
            for k in range(32):
                moves[m, q * 32 + k, q * 128 + m * 32 + k] = 1.0
    return moves


def tag_picks():
    rows = np.zeros((2, 2, SPAN, ROWS * LEVELS), np.float32)
    cols = np.zeros((2, SPAN, COLS), np.float32)
    for n, (part, a, o) in enumerate(positions(BOTH, range(6), range(12))):
        for half in range(2):
            cols[half, n, 12 * half + o] = 1.0
            for pair in range(2):
                rows[half, pair, n, (6 * half + a) * LEVELS + 2 * pair + part] = 1.0
    return rows, cols


SLABS = {0: (208, 80), 1: (64, 160), 2: (208, 80), 3: (64, 160)}


def place(w, pair):
    return pair * 2 + w if w < 2 else w * 2 + pair


def own_level(pair, part):
    return (2 * pair + part + 1) % LEVELS


def nn(a, b):
    return lax.dot_general(a, b, (((1,), (0,)), ((), ())), preferred_element_type=F32)


def tn(a, b):
    return lax.dot_general(a, b, (((0,), (0,)), ((), ())), preferred_element_type=F32)


def nt(a, b):
    return lax.dot_general(a, b, (((1,), (1,)), ((), ())), preferred_element_type=F32)


def kernel(
    tokens_in, region_in, qkv_in, proj_in, packs_in, gathers_in, sides_in, moves_in, packs_t_in, gathers_t_in,
    sides_t_in, pick_rows_in, pick_cols_in,
    restored_out, proj_out,
    tokens, region, qkv_part, proj_part, packs, gathers, sides, moves, packs_t, gathers_t, sides_t, pick_rows, pick_cols,
    ids, tag_rows, tag_cols, normed, windows, qkv, attended, restored, given, raw, whole_qkv, whole_proj,
    w_out, n_out, c_out, w_in, n_in, c_in, w_back, n_back, c_back, w_home, n_home, c_home,
    in_sem, out_sem,
    z_send, z_recv, p_send, p_recv, core_send, core_recv, halo_send, halo_recv, back_send, back_recv,
):
    lat = lax.axis_index("lat")
    lon = lax.axis_index("lon")
    core = lat % 2
    y = (lat // 2) % 4
    x = (lon % 2) * 2 + lat // 8
    z = lon // 2

    def at(xx, yy, zz, cc):
        return ((xx % 2) * 8 + yy * 2 + cc, zz * 2 + xx // 2)

    def along_z(step):
        return at(x, y, (z + step + 16) % 16, core)

    def one_way(d):
        return at((x + d) % 4, y, z, core)

    def other_way(d):
        return at(x, (y + d) % 4, z, core)

    def beside(d_lat, d_lon):
        return ((lat + d_lat + 16) % 16, (lon + d_lon + 32) % 32)

    peer = at(x, y, z, 1 - core)
    near = [s for s in RELATIVE if 0 < abs(s) <= 4]
    partners = [along_z(s) for s in near]
    partners += [one_way(d) for d in (1, 2, 3)] + [other_way(d) for d in (1, 2, 3)] + [peer]
    partners += [beside(a, b) for a, b in ((0, 1), (0, -1), (1, 0), (-1, 0), (1, 1), (-1, -1))]
    barrier = pltpu.get_barrier_semaphore()
    for partner in partners:
        pl.semaphore_signal(barrier, 1, device_id=partner, device_id_type=MESH)

    loads = [
        pltpu.make_async_copy(src, dst, in_sem.at[n])
        for n, (src, dst) in enumerate((
            (qkv_in, qkv_part), (proj_in, proj_part), (tokens_in, tokens), (packs_in, packs), (region_in, region),
            (pick_rows_in, pick_rows), (pick_cols_in, pick_cols), (gathers_in, gathers), (sides_in, sides),
            (moves_in, moves), (sides_t_in, sides_t), (gathers_t_in, gathers_t), (packs_t_in, packs_t),
        ))
    ]
    for load in loads:
        load.start()

    loads[0].wait()
    loads[1].wait()
    line = lax.broadcasted_iota(jnp.int32, (32, 128), 0)
    lane = lax.broadcasted_iota(jnp.int32, (32, 128), 1)
    total = 0.0
    for q in range(4):
        spot = jnp.where(lane == line + 32 * q, 1.0, 0.0).astype(BF16)
        if q < 3:
            total += tn(qkv_part[...], spot)[q * 16:(q + 1) * 16]
        else:
            total += nn(proj_part[...], spot)
    raw[0, 0, 0, 0] = total.astype(BF16)

    pl.semaphore_wait(barrier, len(partners))

    def remote(src, dst, send, recv, target):
        return pltpu.make_async_remote_copy(src, dst, send, recv, device_id=target, device_id_type=MESH)

    first = []
    for n, s in enumerate(near):
        slot = RELATIVE.index(-s)
        copy = remote(raw.at[0, 0, 0, 0], raw.at[0, 0, 0, slot], z_send.at[n], z_recv.at[slot], along_z(s))
        copy.start()
        first.append(copy)
    loads[2].wait()

    @pl.loop(0, LEVELS)
    def _(i):
        rows = pl.ds(pl.multiple_of(i * LEVEL, LEVEL), LEVEL)
        floated = tokens[rows, :].astype(F32)
        average = jnp.mean(floated, axis=-1, keepdims=True)
        centred = floated - average
        spread = jnp.mean(centred * centred, axis=-1, keepdims=True)
        normed[rows, :] = (centred * lax.rsqrt(spread + EPS)).astype(BF16)

    def slab(pair, part, start, size):
        return normed[pl.ds(own_level(pair, part) * LEVEL + start, size), :]

    loads[3].wait()
    for pair in range(2):
        for buf, begins, size, start, height in (
            (w_out, 0, 112, 64, 224), (n_out, 112, 112, 0, 80), (c_out, 224, 48, 0, 80),
        ):
            total = 0.0
            for part in range(2):
                chosen = packs[pl.ds(begins, size), pl.ds(part * LEVEL, LEVEL)][:, start:start + height]
                total += nn(chosen, slab(pair, part, start, height))
            buf[pl.ds(pair * size, size), :] = total.astype(BF16)

    halos = []

    def send_halo(n, pair):
        src, dst, size, target = (
            (w_out, w_in, 112, beside(0, -1)), (n_out, n_in, 112, beside(-1, 0)), (c_out, c_in, 48, beside(-1, -1)),
        )[n]
        rows = pl.ds(pair * size, size)
        copy = remote(src.at[rows, :], dst.at[rows, :], halo_send.at[n, pair], halo_recv.at[n, pair], target)
        copy.start()
        halos.append(copy)

    send_halo(0, 0)
    send_halo(2, 0)
    send_halo(1, 0)
    send_halo(1, 1)
    for copy in first:
        copy.wait_recv()

    far = [
        remote(raw.at[0, 0, 0, pl.ds(1, 4)], raw.at[0, 0, 0, pl.ds(9, 4)], z_send.at[8], z_recv.at[9], along_z(-4)),
        remote(raw.at[0, 0, 0, pl.ds(5, 3)], raw.at[0, 0, 0, pl.ds(13, 3)], z_send.at[9], z_recv.at[10], along_z(4)),
    ]
    for copy in far:
        copy.start()

    def step_one(part, d):
        span = pl.ds(*PARTS[part])
        return remote(
            raw.at[0, 0, 0, span], raw.at[0, 4 - d, 0, span], p_send.at[part, d, 0], p_recv.at[part, 4 - d, 0], one_way(d)
        )

    def step_two(part, i, d):
        span = pl.ds(*PARTS[part])
        return remote(
            raw.at[0, i, 0, span], raw.at[0, i, 4 - d, span], p_send.at[part, i, d], p_recv.at[part, i, 4 - d], other_way(d)
        )

    def arrival(part, i, k):
        span = pl.ds(*PARTS[part])
        return remote(
            raw.at[0, 0, 0, span], raw.at[0, i, k, span], p_send.at[part, i, k], p_recv.at[part, i, k], peer
        )

    def relay(part, i, k):
        span = pl.ds(*PARTS[part])
        return remote(
            raw.at[0, i, k, span], raw.at[1, i, k, span], core_send.at[part, i, k], core_recv.at[part, i, k], peer
        )

    def begin(part):
        for d in (1, 3, 2):
            step_one(part, d).start()
        for d in (1, 3, 2):
            step_two(part, 0, d).start()
        relay(part, 0, 0).start()

    def forward(part):
        for i in (1, 3, 2):
            arrival(part, i, 0).wait_recv()
            for d in (1, 3, 2):
                step_two(part, i, d).start()
            relay(part, i, 0).start()

    def pass_on(part, i):
        for k in (1, 3, 2):
            arrival(part, i, k).wait_recv()
            relay(part, i, k).start()

    def unpack(part):
        @pl.loop(0, 4)
        def _(i):
            for k in range(4):
                relay(part, i, k).wait_recv()

        start, count = PARTS[part]
        for x_hi in range(2):
            for group in range(4):
                x_lo, y_hi = group // 2, group % 2
                total = 0.0
                for member in range(4):
                    y_lo, cc = member // 2, member % 2
                    d_x, d_y = (x_hi * 2 + x_lo - x + 4) % 4, (y_hi * 2 + y_lo - y + 4) % 4
                    piece = raw[(cc + core) % 2, d_x, d_y, pl.ds(start, count)].reshape(count * 16, 128)
                    total += nn(piece, moves[member])
                total = total.astype(BF16)
                lanes = pl.ds(group * 128, 128)
                for s in range(count):
                    band = ((z + RELATIVE[start + s] + 16) % 16) * 2 + x_hi
                    for q in range(4):
                        block = total[s * 16:(s + 1) * 16, q * 128:(q + 1) * 128]
                        if q < 3:
                            whole_qkv[pl.ds(pl.multiple_of(band * 48 + q * 16, 16), 16), lanes] = block
                        else:
                            whole_proj[pl.ds(pl.multiple_of(band * 16, 16), 16), lanes] = block

    begin(0)
    for n in (4, 5, 6):
        loads[n].wait()
    for a in range(ROWS):
        ids[pl.ds(a * LEVELS, LEVELS), :] = region[a].astype(F32)
    for w in range(4):
        half_lat, half_lon = (1, 0, 1, 0)[w], (1, 1, 0, 0)[w]
        for pair in range(2):
            column = nn(pick_rows[half_lat, pair], ids[...].astype(BF16))
            column = jnp.sum(column * pick_cols[half_lon].astype(F32), axis=-1, keepdims=True)
            square = (SPAN, SPAN)
            same = lax.broadcasted_iota(jnp.int32, square, 0) == lax.broadcasted_iota(jnp.int32, square, 1)
            spots = jnp.where(same, column, 0.0).astype(BF16)
            tag_cols[place(w, pair)] = column
            tag_rows[place(w, pair)] = nn(jnp.ones((8, SPAN), BF16), spots)

    forward(0)
    for copy in far:
        copy.wait_recv()
    begin(1)
    send_halo(0, 1)
    send_halo(2, 1)
    pass_on(0, 0)
    forward(1)

    @pl.loop(1, 4)
    def _(i):
        pass_on(0, i)

    loads[7].wait()
    loads[8].wait()
    for copy in halos:
        copy.wait_recv()
    sizes = (112, 112, 48)
    for pair in range(2):
        for w in range(4):
            start, height = SLABS[w]
            total = 0.0
            for part in range(2):
                chosen = gathers[w, :, pl.ds(part * LEVEL, LEVEL)][:, start:start + height]
                total += nn(chosen, slab(pair, part, start, height))
            for k, arrived in enumerate((w_in, n_in, c_in)):
                if SIDES[w][k] is not None:
                    total += nn(
                        sides[w, :, pl.ds(k * 128, sizes[k])], arrived[pl.ds(pair * sizes[k], sizes[k]), :]
                    )
            windows[pl.ds(place(w, pair) * SPAN, SPAN), :] = total.astype(BF16)

    pass_on(1, 0)
    loads[9].wait()
    unpack(0)

    @pl.loop(1, 4)
    def _(i):
        pass_on(1, i)

    unpack(1)
    proj_copy = pltpu.make_async_copy(whole_proj, proj_out, out_sem.at[4])
    proj_copy.start()

    def project_in(start, count):
        rows = pl.ds(start * SPAN, count * SPAN)
        for n in range(6):
            qkv[n, rows, :] = nt(windows[rows, :], whole_qkv[pl.ds(n * 256, 256), :]).astype(BF16)

    lower = lax.broadcasted_iota(jnp.int32, (SPAN, 128), 1) < 64
    ones = jnp.ones((SPAN, 128), BF16)

    def attend(w):
        rows = pl.ds(pl.multiple_of(w * SPAN, 16), SPAN)
        bias = jnp.where(tag_cols[w] == tag_rows[w][0:1], 0.0, -1e30)
        bias = jnp.concatenate([bias, bias], axis=0)
        scores = []
        for t in range(4):
            lanes = slice((t % 2) * 128, (t % 2) * 128 + 128)
            query = qkv[t // 2, rows, lanes]
            zero = jnp.zeros_like(query)
            both = jnp.concatenate([jnp.where(lower, query, zero), jnp.where(lower, zero, query)], axis=0)
            scores.append(nt(both, qkv[2 + t // 2, rows, lanes]) + bias)
        raised = [
            jnp.exp2((score - jnp.max(score, axis=-1, keepdims=True)) * SCALE).astype(BF16) for score in scores
        ]
        for t in range(4):
            lanes = slice((t % 2) * 128, (t % 2) * 128 + 128)
            mixed = nn(raised[t], jnp.concatenate([qkv[4 + t // 2, rows, lanes], ones], axis=1))
            top = jnp.where(lower, mixed[:SPAN, :128], mixed[SPAN:, :128])
            bottom = jnp.where(lower, mixed[:SPAN, 128:], mixed[SPAN:, 128:])
            attended[w, :, pl.ds(t * 128, 128)] = (top / bottom).astype(BF16)

    returns = []

    def give_back(k, sources, pair, target):
        total = 0.0
        for w in sources:
            total += nn(sides_t[w, pl.ds(k * 128, sizes[k]), :], attended[place(w, pair)])
        rows = pl.ds(pair * sizes[k], sizes[k])
        src, dst = ((w_back, w_home), (n_back, n_home), (c_back, c_home))[k]
        src[rows, :] = total.astype(BF16)
        copy = remote(src.at[rows, :], dst.at[rows, :], back_send.at[k, pair], back_recv.at[k, pair], target)
        copy.start()
        returns.append(copy)

    loads[10].wait()
    for pair in range(2):
        project_in(2 * pair, 2)

        @pl.loop(2 * pair, 2 * pair + 2)
        def _(w):
            attend(w)

        give_back(0, (0, 1), pair, beside(0, 1))
        give_back(2, (0,), pair, beside(1, 1))

    project_in(4, 4)

    @pl.loop(4, 6)
    def _(w):
        attend(w)

    for pair in range(2):
        give_back(1, (0, 2), pair, beside(1, 0))

    @pl.loop(6, 8)
    def _(w):
        attend(w)

    loads[11].wait()
    for pair in range(2):
        for part in range(2):
            total = 0.0
            for w in range(4):
                total += nn(gathers_t[w, pl.ds(part * LEVEL, LEVEL), :], attended[place(w, pair)])
            restored[own_level(pair, part)] = total

    loads[12].wait()
    for copy in returns:
        copy.wait_recv()
    written = [proj_copy]
    for pair in range(2):
        for part in range(2):
            level = own_level(pair, part)
            total = restored[level]
            for k, home in enumerate((w_home, n_home, c_home)):
                total += nn(
                    packs_t[pl.ds(part * LEVEL, LEVEL), pl.ds(k * 128, sizes[k])],
                    home[pl.ds(pair * sizes[k], sizes[k]), :],
                )
            rows = pl.ds(level * LEVEL, LEVEL)
            given[rows, :] = total.astype(BF16)
            copy = pltpu.make_async_copy(given.at[rows, :], restored_out.at[rows, :], out_sem.at[level])
            copy.start()
            written.append(copy)

    for copy in first + far + halos + returns:
        copy.wait_send()
    for part in range(2):
        for d in (1, 2, 3):
            step_one(part, d).wait_send()

        @pl.loop(0, 4)
        def _(i):
            for d in (1, 2, 3):
                step_two(part, i, d).wait_send()
            for k in range(4):
                relay(part, i, k).wait_send()

    for copy in written:
        copy.wait()


def constants():
    packs = np.concatenate(PACKS, axis=0)
    gathers = np.stack(GATHERS)
    sides = np.zeros((3, SPAN, 384), np.float32)
    for w in range(3):
        for k, matrix in enumerate(SIDES[w]):
            if matrix is not None:
                sides[w, :, k * 128:k * 128 + matrix.shape[1]] = matrix
    packs_t = np.zeros((2 * LEVEL, 384), np.float32)
    for k, matrix in enumerate(PACKS):
        packs_t[:, k * 128:k * 128 + matrix.shape[0]] = matrix.T
    pick_rows, pick_cols = tag_picks()
    return [
        jnp.asarray(a, BF16)
        for a in (
            packs, gathers, sides, lane_moves(), packs_t, gathers.transpose(0, 2, 1), sides.transpose(0, 2, 1),
            pick_rows, pick_cols,
        )
    ]


def local(tokens, region, qkv_weight, proj_weight):
    flat = tokens.reshape(-1, D)
    operands = [flat, region.transpose(1, 0, 2), qkv_weight, proj_weight.T, *constants()]
    operands = [pltpu.with_memory_space_constraint(a, pltpu.HBM) for a in operands]
    anywhere = pl.BlockSpec(memory_space=pl.ANY)
    dma = pltpu.SemaphoreType.DMA

    def pieces():
        return [pltpu.VMEM((n, D), BF16) for n in (224, 224, 96)]

    restored, whole_proj = pl.pallas_call(
        kernel,
        out_shape=[jax.ShapeDtypeStruct(flat.shape, BF16), jax.ShapeDtypeStruct((D, D), BF16)],
        in_specs=[anywhere] * len(operands),
        out_specs=[anywhere] * 2,
        scratch_shapes=[
            *[pltpu.VMEM(a.shape, a.dtype) for a in operands],
            pltpu.VMEM((ROWS * LEVELS, COLS), F32),
            pltpu.VMEM((8, 8, SPAN), F32),
            pltpu.VMEM((8, SPAN, 1), F32),
            pltpu.VMEM((LEVELS * LEVEL, D), BF16),
            pltpu.VMEM((8 * SPAN, D), BF16),
            pltpu.VMEM((6, 8 * SPAN, 256), BF16),
            pltpu.VMEM((8, SPAN, D), BF16),
            pltpu.VMEM((LEVELS, LEVEL, D), F32),
            pltpu.VMEM((LEVELS * LEVEL, D), BF16),
            pltpu.VMEM((2, 4, 4, 16, 16, 128), BF16),
            pltpu.VMEM((3 * D, D), BF16),
            pltpu.VMEM((D, D), BF16),
            *pieces(), *pieces(), *pieces(), *pieces(),
            dma((len(operands),)), dma((5,)),
            dma((10,)), dma((11,)), dma((2, 4, 4)), dma((2, 4, 4)), dma((2, 4, 4)), dma((2, 4, 4)),
            dma((3, 2)), dma((3, 2)), dma((3, 2)), dma((3, 2)),
        ],
        compiler_params=pltpu.CompilerParams(
            collective_id=0, has_side_effects=True, vmem_limit_bytes=34 * 1024 * 1024
        ),
        name="attention_block",
    )(*operands)
    blended = flat.astype(F32) + nt(restored, whole_proj)
    return blended.astype(BF16).reshape(tokens.shape)


def solution(mesh):
    placed = (P(None, "lat", "lon", None), P(None, "lat", "lon"), P("lat", "lon"), P("lat", "lon"))
    return jax.shard_map(
        local, mesh=mesh, in_specs=placed, out_specs=P(None, "lat", "lon", None), check_vma=False
    )
```

```python
import jax
import jax.numpy as jnp
import numpy as np
from jax import lax
from jax.experimental import pallas as pl
from jax.experimental.pallas import tpu as pltpu
from jax.sharding import PartitionSpec as P

MESH = pl.DeviceIdType.MESH
BF16 = jnp.bfloat16
F32 = jnp.float32

LEVELS, ROWS, COLS, D = 4, 12, 24, 512
HEADS = 8
LEVEL = ROWS * COLS
SPAN = 144
EPS = 1e-05
SCALE = float(np.log2(np.e) / 8.0)

RELATIVE = [0, 1, 2, 3, 4, -1, -2, -3, -4, 5, 6, 7, 8, -5, -6, -7]
PARTS = ((0, 9), (9, 7))


def positions(levels, rows, cols, pad=0):
    found = [(l, a, o) for l in levels for a in rows for o in cols]
    return found + [None] * pad


def one_hot(dest, source):
    where = {place: i for i, place in enumerate(source) if place is not None}
    matrix = np.zeros((len(dest), len(source)), np.float32)
    for i, place in enumerate(dest):
        if place in where:
            matrix[i, where[place]] = 1.0
    return matrix


BOTH = (0, 1)
OWN = positions(BOTH, range(ROWS), range(COLS))
W_PACK = positions(BOTH, range(3, 12), range(6), 4)
N_PACK = positions(BOTH, range(3), range(6, 24), 4)
C_PACK = positions(BOTH, range(3), range(6), 12)
E_SIDE = positions(BOTH, range(3, 12), range(24, 30), 4)
S_SIDE = positions(BOTH, range(12, 15), range(6, 24), 4)
C_SIDE = positions(BOTH, range(12, 15), range(24, 30), 12)
WINDOWS = [
    positions(BOTH, range(3 + 6 * i, 9 + 6 * i), range(6 + 12 * j, 18 + 12 * j))
    for j in (1, 0)
    for i in (1, 0)
]

PACKS = [one_hot(pack, OWN) for pack in (W_PACK, N_PACK, C_PACK)]
GATHERS = [one_hot(window, OWN) for window in WINDOWS]
SIDES = [
    [one_hot(WINDOWS[0], E_SIDE), one_hot(WINDOWS[0], S_SIDE), one_hot(WINDOWS[0], C_SIDE)],
    [one_hot(WINDOWS[1], E_SIDE), None, None],
    [None, one_hot(WINDOWS[2], S_SIDE), None],
    [None, None, None],
]


def lane_moves():
    moves = np.zeros((4, 128, 512), np.float32)
    for m in range(4):
        for q in range(4):
            for k in range(32):
                moves[m, q * 32 + k, q * 128 + m * 32 + k] = 1.0
    return moves


def tag_picks():
    rows = np.zeros((2, 2, SPAN, ROWS * LEVELS), np.float32)
    cols = np.zeros((2, SPAN, COLS), np.float32)
    for n, (part, a, o) in enumerate(positions(BOTH, range(6), range(12))):
        for half in range(2):
            cols[half, n, 12 * half + o] = 1.0
            for pair in range(2):
                rows[half, pair, n, (6 * half + a) * LEVELS + 2 * pair + part] = 1.0
    return rows, cols


SLABS = {0: (208, 80), 1: (64, 160), 2: (208, 80), 3: (64, 160)}


def place(w, pair):
    return pair * 2 + w if w < 2 else w * 2 + pair


def own_level(pair, part):
    return (2 * pair + part + 1) % LEVELS


def nn(a, b):
    return lax.dot_general(a, b, (((1,), (0,)), ((), ())), preferred_element_type=F32)


def tn(a, b):
    return lax.dot_general(a, b, (((0,), (0,)), ((), ())), preferred_element_type=F32)


def nt(a, b):
    return lax.dot_general(a, b, (((1,), (1,)), ((), ())), preferred_element_type=F32)


def kernel(
    tokens_in, region_in, qkv_in, proj_in, packs_in, gathers_in, sides_in, moves_in, packs_t_in, gathers_t_in,
    sides_t_in, pick_rows_in, pick_cols_in,
    restored_out, proj_out,
    tokens, region, qkv_part, proj_part, packs, gathers, sides, moves, packs_t, gathers_t, sides_t, pick_rows, pick_cols,
    ids, tag_rows, tag_cols, normed, windows, qkv, attended, restored, given, raw, whole_qkv, whole_proj,
    w_out, n_out, c_out, w_in, n_in, c_in, w_back, n_back, c_back, w_home, n_home, c_home,
    in_sem, out_sem,
    z_send, z_recv, p_send, p_recv, core_send, core_recv, halo_send, halo_recv, back_send, back_recv,
):
    lat = lax.axis_index("lat")
    lon = lax.axis_index("lon")
    core = lat % 2
    y = (lat // 2) % 4
    x = (lon % 2) * 2 + lat // 8
    z = lon // 2

    def at(xx, yy, zz, cc):
        return ((xx % 2) * 8 + yy * 2 + cc, zz * 2 + xx // 2)

    def along_z(step):
        return at(x, y, (z + step + 16) % 16, core)

    def one_way(part, d):
        turn = part * core
        return at((x + d * (1 - turn)) % 4, (y + d * turn) % 4, z, core)

    def other_way(part, d):
        turn = part * core
        return at((x + d * turn) % 4, (y + d * (1 - turn)) % 4, z, core)

    def beside(d_lat, d_lon):
        return ((lat + d_lat + 16) % 16, (lon + d_lon + 32) % 32)

    peer = at(x, y, z, 1 - core)
    near = [4, -4, 3, -3, 2, -2, 1, -1]
    loads = [
        pltpu.make_async_copy(src, dst, in_sem.at[n])
        for n, (src, dst) in enumerate((
            (qkv_in, qkv_part), (proj_in, proj_part), (tokens_in, tokens), (packs_in, packs), (region_in, region),
            (pick_rows_in, pick_rows), (pick_cols_in, pick_cols), (gathers_in, gathers), (sides_in, sides),
            (moves_in, moves), (sides_t_in, sides_t), (gathers_t_in, gathers_t), (packs_t_in, packs_t),
        ))
    ]
    for load in loads[:2]:
        load.start()

    partners = [along_z(s) for s in near]
    partners += [one_way(0, d) for d in (1, 2, 3)] + [other_way(0, d) for d in (1, 2, 3)] + [peer]
    partners += [beside(a, b) for a, b in ((0, 1), (0, -1), (1, 0), (-1, 0), (1, 1), (-1, -1))]
    barrier = pltpu.get_barrier_semaphore()
    for partner in partners:
        pl.semaphore_signal(barrier, 1, device_id=partner, device_id_type=MESH)

    for load in loads[2:]:
        load.start()

    loads[0].wait()
    loads[1].wait()
    line = lax.broadcasted_iota(jnp.int32, (32, 128), 0)
    lane = lax.broadcasted_iota(jnp.int32, (32, 128), 1)
    total = 0.0
    for q in range(4):
        spot = jnp.where(lane == line + 32 * q, 1.0, 0.0).astype(BF16)
        if q < 3:
            total += tn(qkv_part[...], spot)[q * 16:(q + 1) * 16]
        else:
            total += nn(proj_part[...], spot)
    raw[0, 0, 0, 0] = total.astype(BF16)

    pl.semaphore_wait(barrier, len(partners))

    def remote(src, dst, send, recv, target):
        return pltpu.make_async_remote_copy(src, dst, send, recv, device_id=target, device_id_type=MESH)

    first = []
    for n, s in enumerate(near):
        slot = RELATIVE.index(-s)
        copy = remote(raw.at[0, 0, 0, 0], raw.at[0, 0, 0, slot], z_send.at[n], z_recv.at[slot], along_z(s))
        copy.start()
        first.append(copy)
    loads[2].wait()

    @pl.loop(0, LEVELS)
    def _(i):
        rows = pl.ds(pl.multiple_of(i * LEVEL, LEVEL), LEVEL)
        floated = tokens[rows, :].astype(F32)
        average = jnp.mean(floated, axis=-1, keepdims=True)
        centred = floated - average
        spread = jnp.mean(centred * centred, axis=-1, keepdims=True)
        normed[rows, :] = (centred * lax.rsqrt(spread + EPS)).astype(BF16)

    def slab(pair, part, start, size):
        return normed[pl.ds(own_level(pair, part) * LEVEL + start, size), :]

    loads[3].wait()
    for pair in range(2):
        for buf, begins, size, start, height in (
            (w_out, 0, 112, 64, 224), (n_out, 112, 112, 0, 80), (c_out, 224, 48, 0, 80),
        ):
            total = 0.0
            for part in range(2):
                chosen = packs[pl.ds(begins, size), pl.ds(part * LEVEL, LEVEL)][:, start:start + height]
                total += nn(chosen, slab(pair, part, start, height))
            buf[pl.ds(pair * size, size), :] = total.astype(BF16)

    halos = {}

    def send_halo(n, pair):
        src, dst, size, target = (
            (w_out, w_in, 112, beside(0, -1)), (n_out, n_in, 112, beside(-1, 0)), (c_out, c_in, 48, beside(-1, -1)),
        )[n]
        rows = pl.ds(pair * size, size)
        copy = remote(src.at[rows, :], dst.at[rows, :], halo_send.at[n, pair], halo_recv.at[n, pair], target)
        copy.start()
        halos[n, pair] = copy

    send_halo(0, 0)
    send_halo(2, 0)
    send_halo(1, 0)
    send_halo(1, 1)
    for copy in first:
        copy.wait_recv()

    far = [
        remote(raw.at[0, 0, 0, pl.ds(1, 4)], raw.at[0, 0, 0, pl.ds(9, 4)], z_send.at[8], z_recv.at[9], along_z(-4)),
        remote(raw.at[0, 0, 0, pl.ds(5, 3)], raw.at[0, 0, 0, pl.ds(13, 3)], z_send.at[9], z_recv.at[10], along_z(4)),
    ]
    for copy in far:
        copy.start()

    def step_one(part, d):
        span = pl.ds(*PARTS[part])
        return remote(
            raw.at[0, 0, 0, span], raw.at[0, 4 - d, 0, span], p_send.at[part, d, 0], p_recv.at[part, 4 - d, 0], one_way(part, d)
        )

    def step_two(part, i, d):
        span = pl.ds(*PARTS[part])
        return remote(
            raw.at[0, i, 0, span], raw.at[0, i, 4 - d, span], p_send.at[part, i, d], p_recv.at[part, i, 4 - d], other_way(part, d)
        )

    def arrival(part, i, k):
        span = pl.ds(*PARTS[part])
        return remote(
            raw.at[0, 0, 0, span], raw.at[0, i, k, span], p_send.at[part, i, k], p_recv.at[part, i, k], peer
        )

    def relay(part, i, k):
        span = pl.ds(*PARTS[part])
        return remote(
            raw.at[0, i, k, span], raw.at[1, i, k, span], core_send.at[part, i, k], core_recv.at[part, i, k], peer
        )

    def begin(part):
        for d in (2, 1, 3):
            step_one(part, d).start()
        for d in (2, 1, 3):
            step_two(part, 0, d).start()
        relay(part, 0, 0).start()

    def forward(part):
        for i in (1, 3, 2):
            arrival(part, i, 0).wait_recv()
            for d in (2, 1, 3):
                step_two(part, i, d).start()
            relay(part, i, 0).start()

    def pass_on(part, i):
        for k in (1, 3, 2):
            arrival(part, i, k).wait_recv()
            relay(part, i, k).start()

    def unpack(part):
        @pl.loop(0, 4)
        def _(i):
            for k in range(4):
                relay(part, i, k).wait_recv()

        start, count = PARTS[part]
        for x_hi in range(2):
            for group in range(4):
                x_lo, y_hi = group // 2, group % 2
                total = 0.0
                for member in range(4):
                    y_lo, cc = member // 2, member % 2
                    d_x, d_y = (x_hi * 2 + x_lo - x + 4) % 4, (y_hi * 2 + y_lo - y + 4) % 4
                    i, k = (d_y, d_x) if part * cc else (d_x, d_y)
                    piece = raw[(cc + core) % 2, i, k, pl.ds(start, count)].reshape(count * 16, 128)
                    total += nn(piece, moves[member])
                total = total.astype(BF16)
                lanes = pl.ds(group * 128, 128)
                for s in range(count):
                    band = ((z + RELATIVE[start + s] + 16) % 16) * 2 + x_hi
                    for q in range(4):
                        block = total[s * 16:(s + 1) * 16, q * 128:(q + 1) * 128]
                        if q < 3:
                            whole_qkv[pl.ds(pl.multiple_of(band * 48 + q * 16, 16), 16), lanes] = block
                        else:
                            whole_proj[pl.ds(pl.multiple_of(band * 16, 16), 16), lanes] = block

    begin(0)
    for n in (4, 5, 6):
        loads[n].wait()
    for a in range(ROWS):
        ids[pl.ds(a * LEVELS, LEVELS), :] = region[a].astype(F32)
    for w in range(4):
        half_lat, half_lon = (1, 0, 1, 0)[w], (1, 1, 0, 0)[w]
        for pair in range(2):
            column = nn(pick_rows[half_lat, pair], ids[...].astype(BF16))
            column = jnp.sum(column * pick_cols[half_lon].astype(F32), axis=-1, keepdims=True)
            square = (SPAN, SPAN)
            same = lax.broadcasted_iota(jnp.int32, square, 0) == lax.broadcasted_iota(jnp.int32, square, 1)
            spots = jnp.where(same, column, 0.0).astype(BF16)
            tag_cols[place(w, pair)] = column
            tag_rows[place(w, pair)] = nn(jnp.ones((8, SPAN), BF16), spots)

    forward(0)
    for copy in far:
        copy.wait_recv()
    begin(1)
    send_halo(0, 1)
    send_halo(2, 1)
    pass_on(0, 0)
    forward(1)

    @pl.loop(1, 4)
    def _(i):
        pass_on(0, i)

    sizes = (112, 112, 48)

    def gather_windows(pair):
        for n in range(3):
            halos[n, pair].wait_recv()
        for w in range(4):
            start, height = SLABS[w]
            total = 0.0
            for part in range(2):
                chosen = gathers[w, :, pl.ds(part * LEVEL, LEVEL)][:, start:start + height]
                total += nn(chosen, slab(pair, part, start, height))
            for k, arrived in enumerate((w_in, n_in, c_in)):
                if SIDES[w][k] is not None:
                    total += nn(
                        sides[w, :, pl.ds(k * 128, sizes[k])], arrived[pl.ds(pair * sizes[k], sizes[k]), :]
                    )
            windows[pl.ds(place(w, pair) * SPAN, SPAN), :] = total.astype(BF16)

    loads[7].wait()
    loads[8].wait()
    gather_windows(0)
    pass_on(1, 0)
    loads[9].wait()
    unpack(0)

    @pl.loop(1, 4)
    def _(i):
        pass_on(1, i)

    gather_windows(1)
    unpack(1)
    proj_copy = pltpu.make_async_copy(whole_proj, proj_out, out_sem.at[4])
    proj_copy.start()

    def project_in(start, count):
        rows = pl.ds(start * SPAN, count * SPAN)
        for n in range(6):
            qkv[n, rows, :] = nt(windows[rows, :], whole_qkv[pl.ds(n * 256, 256), :]).astype(BF16)

    lower = lax.broadcasted_iota(jnp.int32, (SPAN, 128), 1) < 64
    ones = jnp.ones((SPAN, 128), BF16)

    def attend(w):
        rows = pl.ds(pl.multiple_of(w * SPAN, 16), SPAN)
        bias = jnp.where(tag_cols[w] == tag_rows[w][0:1], 0.0, -1e30)
        bias = jnp.concatenate([bias, bias], axis=0)
        scores = []
        for t in range(4):
            lanes = slice((t % 2) * 128, (t % 2) * 128 + 128)
            query = qkv[t // 2, rows, lanes]
            zero = jnp.zeros_like(query)
            both = jnp.concatenate([jnp.where(lower, query, zero), jnp.where(lower, zero, query)], axis=0)
            scores.append(nt(both, qkv[2 + t // 2, rows, lanes]) + bias)
        raised = [
            jnp.exp2((score - jnp.max(score, axis=-1, keepdims=True)) * SCALE).astype(BF16) for score in scores
        ]
        for t in range(4):
            lanes = slice((t % 2) * 128, (t % 2) * 128 + 128)
            mixed = nn(raised[t], jnp.concatenate([qkv[4 + t // 2, rows, lanes], ones], axis=1))
            top = jnp.where(lower, mixed[:SPAN, :128], mixed[SPAN:, :128])
            bottom = jnp.where(lower, mixed[:SPAN, 128:], mixed[SPAN:, 128:])
            attended[w, :, pl.ds(t * 128, 128)] = (top / bottom).astype(BF16)

    returns = {}

    def give_back(k, sources, pair, target):
        total = 0.0
        for w in sources:
            total += nn(sides_t[w, pl.ds(k * 128, sizes[k]), :], attended[place(w, pair)])
        rows = pl.ds(pair * sizes[k], sizes[k])
        src, dst = ((w_back, w_home), (n_back, n_home), (c_back, c_home))[k]
        src[rows, :] = total.astype(BF16)
        copy = remote(src.at[rows, :], dst.at[rows, :], back_send.at[k, pair], back_recv.at[k, pair], target)
        copy.start()
        returns[k, pair] = copy

    loads[10].wait()
    for pair in range(2):
        project_in(2 * pair, 2)

        @pl.loop(2 * pair, 2 * pair + 2, unroll=2)
        def _(w):
            attend(w)

        give_back(0, (0, 1), pair, beside(0, 1))
        give_back(2, (0,), pair, beside(1, 1))

    project_in(4, 4)

    @pl.loop(4, 6, unroll=2)
    def _(w):
        attend(w)

    for pair in range(2):
        give_back(1, (0, 2), pair, beside(1, 0))

    @pl.loop(6, 8, unroll=2)
    def _(w):
        attend(w)

    loads[11].wait()
    for pair in range(2):
        for part in range(2):
            total = 0.0
            for w in range(4):
                total += nn(gathers_t[w, pl.ds(part * LEVEL, LEVEL), :], attended[place(w, pair)])
            restored[own_level(pair, part)] = total

    loads[12].wait()
    written = [proj_copy]
    for pair in range(2):
        for k in (1, 2, 0):
            returns[k, pair].wait_recv()
        for part in range(2):
            level = own_level(pair, part)
            total = restored[level]
            for k, home in enumerate((w_home, n_home, c_home)):
                total += nn(
                    packs_t[pl.ds(part * LEVEL, LEVEL), pl.ds(k * 128, sizes[k])],
                    home[pl.ds(pair * sizes[k], sizes[k]), :],
                )
            rows = pl.ds(level * LEVEL, LEVEL)
            given[rows, :] = total.astype(BF16)
            copy = pltpu.make_async_copy(given.at[rows, :], restored_out.at[rows, :], out_sem.at[level])
            copy.start()
            written.append(copy)

    for copy in [*first, *far, *halos.values(), *returns.values()]:
        copy.wait_send()
    for part in range(2):
        for d in (1, 2, 3):
            step_one(part, d).wait_send()

        @pl.loop(0, 4)
        def _(i):
            for d in (1, 2, 3):
                step_two(part, i, d).wait_send()
            for k in range(4):
                relay(part, i, k).wait_send()

    for copy in written:
        copy.wait()


def constants():
    packs = np.concatenate(PACKS, axis=0)
    gathers = np.stack(GATHERS)
    sides = np.zeros((3, SPAN, 384), np.float32)
    for w in range(3):
        for k, matrix in enumerate(SIDES[w]):
            if matrix is not None:
                sides[w, :, k * 128:k * 128 + matrix.shape[1]] = matrix
    packs_t = np.zeros((2 * LEVEL, 384), np.float32)
    for k, matrix in enumerate(PACKS):
        packs_t[:, k * 128:k * 128 + matrix.shape[0]] = matrix.T
    pick_rows, pick_cols = tag_picks()
    return [
        jnp.asarray(a, BF16)
        for a in (
            packs, gathers, sides, lane_moves(), packs_t, gathers.transpose(0, 2, 1), sides.transpose(0, 2, 1),
            pick_rows, pick_cols,
        )
    ]


def local(tokens, region, qkv_weight, proj_weight):
    flat = tokens.reshape(-1, D)
    operands = [flat, region.transpose(1, 0, 2), qkv_weight, proj_weight.T, *constants()]
    operands = [pltpu.with_memory_space_constraint(a, pltpu.HBM) for a in operands]
    anywhere = pl.BlockSpec(memory_space=pl.ANY)
    dma = pltpu.SemaphoreType.DMA

    def pieces():
        return [pltpu.VMEM((n, D), BF16) for n in (224, 224, 96)]

    restored, whole_proj = pl.pallas_call(
        kernel,
        out_shape=[jax.ShapeDtypeStruct(flat.shape, BF16), jax.ShapeDtypeStruct((D, D), BF16)],
        in_specs=[anywhere] * len(operands),
        out_specs=[anywhere] * 2,
        scratch_shapes=[
            *[pltpu.VMEM(a.shape, a.dtype) for a in operands],
            pltpu.VMEM((ROWS * LEVELS, COLS), F32),
            pltpu.VMEM((8, 8, SPAN), F32),
            pltpu.VMEM((8, SPAN, 1), F32),
            pltpu.VMEM((LEVELS * LEVEL, D), BF16),
            pltpu.VMEM((8 * SPAN, D), BF16),
            pltpu.VMEM((6, 8 * SPAN, 256), BF16),
            pltpu.VMEM((8, SPAN, D), BF16),
            pltpu.VMEM((LEVELS, LEVEL, D), F32),
            pltpu.VMEM((LEVELS * LEVEL, D), BF16),
            pltpu.VMEM((2, 4, 4, 16, 16, 128), BF16),
            pltpu.VMEM((3 * D, D), BF16),
            pltpu.VMEM((D, D), BF16),
            *pieces(), *pieces(), *pieces(), *pieces(),
            dma((len(operands),)), dma((5,)),
            dma((10,)), dma((11,)), dma((2, 4, 4)), dma((2, 4, 4)), dma((2, 4, 4)), dma((2, 4, 4)),
            dma((3, 2)), dma((3, 2)), dma((3, 2)), dma((3, 2)),
        ],
        compiler_params=pltpu.CompilerParams(
            collective_id=0, has_side_effects=True, vmem_limit_bytes=34 * 1024 * 1024
        ),
        name="attention_block",
    )(*operands)
    blended = flat.astype(F32) + nt(restored, whole_proj)
    return blended.astype(BF16).reshape(tokens.shape)


def solution(mesh):
    placed = (P(None, "lat", "lon", None), P(None, "lat", "lon"), P("lat", "lon"), P("lat", "lon"))
    return jax.shard_map(
        local, mesh=mesh, in_specs=placed, out_specs=P(None, "lat", "lon", None), check_vma=False
    )
```

```python
import jax
import jax.numpy as jnp
import numpy as np
from jax import lax
from jax.experimental import pallas as pl
from jax.experimental.pallas import tpu as pltpu
from jax.sharding import PartitionSpec as P

MESH = pl.DeviceIdType.MESH
BF16 = jnp.bfloat16
F32 = jnp.float32

LEVELS, ROWS, COLS, D = 4, 12, 24, 512
HEADS = 8
LEVEL = ROWS * COLS
SPAN = 144
EPS = 1e-05
SCALE = float(np.log2(np.e) / 8.0)

RELATIVE = [0, 1, 2, 3, 4, -1, -2, -3, -4, 5, 6, 7, 8, -5, -6, -7]
PARTS = ((0, 9), (9, 7))


def positions(levels, rows, cols, pad=0):
    found = [(l, a, o) for l in levels for a in rows for o in cols]
    return found + [None] * pad


def one_hot(dest, source):
    where = {place: i for i, place in enumerate(source) if place is not None}
    matrix = np.zeros((len(dest), len(source)), np.float32)
    for i, place in enumerate(dest):
        if place in where:
            matrix[i, where[place]] = 1.0
    return matrix


BOTH = (0, 1)
OWN = positions(BOTH, range(ROWS), range(COLS))
W_PACK = positions(BOTH, range(3, 12), range(6), 4)
N_PACK = positions(BOTH, range(3), range(6, 24), 4)
C_PACK = positions(BOTH, range(3), range(6), 12)
E_SIDE = positions(BOTH, range(3, 12), range(24, 30), 4)
S_SIDE = positions(BOTH, range(12, 15), range(6, 24), 4)
C_SIDE = positions(BOTH, range(12, 15), range(24, 30), 12)
WINDOWS = [
    positions(BOTH, range(3 + 6 * i, 9 + 6 * i), range(6 + 12 * j, 18 + 12 * j))
    for j in (1, 0)
    for i in (1, 0)
]

PACKS = [one_hot(pack, OWN) for pack in (W_PACK, N_PACK, C_PACK)]
GATHERS = [one_hot(window, OWN) for window in WINDOWS]
SIDES = [
    [one_hot(WINDOWS[0], E_SIDE), one_hot(WINDOWS[0], S_SIDE), one_hot(WINDOWS[0], C_SIDE)],
    [one_hot(WINDOWS[1], E_SIDE), None, None],
    [None, one_hot(WINDOWS[2], S_SIDE), None],
    [None, None, None],
]


def lane_moves():
    moves = np.zeros((4, 128, 512), np.float32)
    for m in range(4):
        for q in range(4):
            for k in range(32):
                moves[m, q * 32 + k, q * 128 + m * 32 + k] = 1.0
    return moves


def tag_picks():
    rows = np.zeros((2, 2, SPAN, ROWS * LEVELS), np.float32)
    cols = np.zeros((2, SPAN, COLS), np.float32)
    for n, (part, a, o) in enumerate(positions(BOTH, range(6), range(12))):
        for half in range(2):
            cols[half, n, 12 * half + o] = 1.0
            for pair in range(2):
                rows[half, pair, n, (6 * half + a) * LEVELS + 2 * pair + part] = 1.0
    return rows, cols


SLABS = {0: (208, 80), 1: (64, 160), 2: (208, 80), 3: (64, 160)}


def place(w, pair):
    return pair * 3 + w if w < 3 else 6 + pair


def own_level(pair, part):
    return (2 * pair + part + 1) % LEVELS


def nn(a, b):
    return lax.dot_general(a, b, (((1,), (0,)), ((), ())), preferred_element_type=F32)


def tn(a, b):
    return lax.dot_general(a, b, (((0,), (0,)), ((), ())), preferred_element_type=F32)


def nt(a, b):
    return lax.dot_general(a, b, (((1,), (1,)), ((), ())), preferred_element_type=F32)


def kernel(
    tokens_in, region_in, qkv_in, proj_in, packs_in, gathers_in, sides_in, moves_in, packs_t_in, gathers_t_in,
    sides_t_in, pick_rows_in, pick_cols_in,
    restored_out, proj_out,
    tokens, region, qkv_part, proj_part, packs, gathers, sides, moves, packs_t, gathers_t, sides_t, pick_rows, pick_cols,
    ids, tag_rows, tag_cols, normed, windows, qkv, attended, restored, given, raw, whole_qkv, whole_proj,
    w_out, n_out, c_out, w_in, n_in, c_in, w_back, n_back, c_back, w_home, n_home, c_home,
    in_sem, out_sem,
    z_send, z_recv, p_send, p_recv, core_send, core_recv, halo_send, halo_recv, back_send, back_recv,
):
    lat = lax.axis_index("lat")
    lon = lax.axis_index("lon")
    core = lat % 2
    y = (lat // 2) % 4
    x = (lon % 2) * 2 + lat // 8
    z = lon // 2

    def at(xx, yy, zz, cc):
        return ((xx % 2) * 8 + yy * 2 + cc, zz * 2 + xx // 2)

    def along_z(step):
        return at(x, y, (z + step + 16) % 16, core)

    def one_way(part, d):
        turn = part * core
        return at((x + d * (1 - turn)) % 4, (y + d * turn) % 4, z, core)

    def other_way(part, d):
        turn = part * core
        return at((x + d * turn) % 4, (y + d * (1 - turn)) % 4, z, core)

    def beside(d_lat, d_lon):
        return ((lat + d_lat + 16) % 16, (lon + d_lon + 32) % 32)

    peer = at(x, y, z, 1 - core)
    near = [4, -4, 3, -3, 2, -2, 1, -1]
    loads = [
        pltpu.make_async_copy(src, dst, in_sem.at[n])
        for n, (src, dst) in enumerate((
            (qkv_in, qkv_part), (proj_in, proj_part), (tokens_in, tokens), (packs_in, packs), (region_in, region),
            (pick_rows_in, pick_rows), (pick_cols_in, pick_cols), (gathers_in, gathers), (sides_in, sides),
            (moves_in, moves), (sides_t_in, sides_t), (gathers_t_in, gathers_t), (packs_t_in, packs_t),
        ))
    ]
    for load in loads[:4]:
        load.start()

    partners = [along_z(s) for s in near]
    partners += [one_way(0, d) for d in (1, 2, 3)] + [other_way(0, d) for d in (1, 2, 3)] + [peer]
    partners += [beside(a, b) for a, b in ((0, 1), (0, -1), (1, 0), (-1, 0), (1, 1), (-1, -1))]
    barrier = pltpu.get_barrier_semaphore()
    for partner in partners:
        pl.semaphore_signal(barrier, 1, device_id=partner, device_id_type=MESH)

    for load in loads[4:]:
        load.start()

    loads[0].wait()
    loads[1].wait()
    line = lax.broadcasted_iota(jnp.int32, (32, 128), 0)
    lane = lax.broadcasted_iota(jnp.int32, (32, 128), 1)
    total = 0.0
    for q in range(4):
        spot = jnp.where(lane == line + 32 * q, 1.0, 0.0).astype(BF16)
        if q < 3:
            total += tn(qkv_part[...], spot)[q * 16:(q + 1) * 16]
        else:
            total += nn(proj_part[...], spot)
    raw[0, 0, 0, 0] = total.astype(BF16)

    pl.semaphore_wait(barrier, len(partners))

    def remote(src, dst, send, recv, target):
        return pltpu.make_async_remote_copy(src, dst, send, recv, device_id=target, device_id_type=MESH)

    first = []
    for n, s in enumerate(near):
        slot = RELATIVE.index(-s)
        copy = remote(raw.at[0, 0, 0, 0], raw.at[0, 0, 0, slot], z_send.at[n], z_recv.at[slot], along_z(s))
        copy.start()
        first.append(copy)
    loads[2].wait()

    def slab(pair, part, start, size):
        return normed[pl.ds(own_level(pair, part) * LEVEL + start, size), :]

    halos = {}

    def send_halo(n, pair):
        src, dst, size, target = (
            (w_out, w_in, 112, beside(0, -1)), (n_out, n_in, 112, beside(-1, 0)), (c_out, c_in, 48, beside(-1, -1)),
        )[n]
        rows = pl.ds(pair * size, size)
        copy = remote(src.at[rows, :], dst.at[rows, :], halo_send.at[n, pair], halo_recv.at[n, pair], target)
        copy.start()
        halos[n, pair] = copy

    loads[3].wait()
    for pair in range(2):

        @pl.loop(0, 2)
        def _(part):
            rows = pl.ds(pl.multiple_of(own_level(pair, part) * LEVEL, LEVEL), LEVEL)
            floated = tokens[rows, :].astype(F32)
            average = jnp.mean(floated, axis=-1, keepdims=True)
            centred = floated - average
            spread = jnp.mean(centred * centred, axis=-1, keepdims=True)
            normed[rows, :] = (centred * lax.rsqrt(spread + EPS)).astype(BF16)

        for buf, begins, size, start, height in (
            (w_out, 0, 112, 64, 224), (c_out, 224, 48, 0, 80), (n_out, 112, 112, 0, 80),
        ):
            total = 0.0
            for part in range(2):
                chosen = packs[pl.ds(begins, size), pl.ds(part * LEVEL, LEVEL)][:, start:start + height]
                total += nn(chosen, slab(pair, part, start, height))
            buf[pl.ds(pair * size, size), :] = total.astype(BF16)
        if pair == 0:
            send_halo(0, 0)
            send_halo(2, 0)
        send_halo(1, pair)

    for copy in first:
        copy.wait_recv()

    far = [
        remote(raw.at[0, 0, 0, pl.ds(1, 4)], raw.at[0, 0, 0, pl.ds(9, 4)], z_send.at[8], z_recv.at[9], along_z(-4)),
        remote(raw.at[0, 0, 0, pl.ds(5, 3)], raw.at[0, 0, 0, pl.ds(13, 3)], z_send.at[9], z_recv.at[10], along_z(4)),
    ]
    for copy in far:
        copy.start()

    def step_one(part, d):
        span = pl.ds(*PARTS[part])
        return remote(
            raw.at[0, 0, 0, span], raw.at[0, 4 - d, 0, span], p_send.at[part, d, 0], p_recv.at[part, 4 - d, 0], one_way(part, d)
        )

    def step_two(part, i, d):
        span = pl.ds(*PARTS[part])
        return remote(
            raw.at[0, i, 0, span], raw.at[0, i, 4 - d, span], p_send.at[part, i, d], p_recv.at[part, i, 4 - d], other_way(part, d)
        )

    def arrival(part, i, k):
        span = pl.ds(*PARTS[part])
        return remote(
            raw.at[0, 0, 0, span], raw.at[0, i, k, span], p_send.at[part, i, k], p_recv.at[part, i, k], peer
        )

    def relay(part, i, k):
        span = pl.ds(*PARTS[part])
        return remote(
            raw.at[0, i, k, span], raw.at[1, i, k, span], core_send.at[part, i, k], core_recv.at[part, i, k], peer
        )

    def begin(part):
        for d in (2, 1, 3):
            step_one(part, d).start()
        for d in (2, 1, 3):
            step_two(part, 0, d).start()
        relay(part, 0, 0).start()

    def forward(part):
        for i in (1, 3, 2):
            arrival(part, i, 0).wait_recv()
            for d in (2, 1, 3):
                step_two(part, i, d).start()
            relay(part, i, 0).start()

    def pass_on(part, i):
        for k in (1, 3, 2):
            arrival(part, i, k).wait_recv()
            relay(part, i, k).start()

    def unpack(part):
        @pl.loop(0, 4)
        def _(i):
            for k in range(4):
                relay(part, i, k).wait_recv()

        start, count = PARTS[part]
        for x_hi in range(2):
            for group in range(4):
                x_lo, y_hi = group // 2, group % 2
                total = 0.0
                for member in range(4):
                    y_lo, cc = member // 2, member % 2
                    d_x, d_y = (x_hi * 2 + x_lo - x + 4) % 4, (y_hi * 2 + y_lo - y + 4) % 4
                    i, k = (d_y, d_x) if part * cc else (d_x, d_y)
                    piece = raw[(cc + core) % 2, i, k, pl.ds(start, count)].reshape(count * 16, 128)
                    total += nn(piece, moves[member])
                total = total.astype(BF16)
                lanes = pl.ds(group * 128, 128)
                for s in range(count):
                    band = ((z + RELATIVE[start + s] + 16) % 16) * 2 + x_hi
                    for q in range(4):
                        block = total[s * 16:(s + 1) * 16, q * 128:(q + 1) * 128]
                        if q < 3:
                            whole_qkv[pl.ds(pl.multiple_of(band * 48 + q * 16, 16), 16), lanes] = block
                        else:
                            whole_proj[pl.ds(pl.multiple_of(band * 16, 16), 16), lanes] = block

    begin(0)
    for n in (4, 5, 6):
        loads[n].wait()
    for a in range(ROWS):
        ids[pl.ds(a * LEVELS, LEVELS), :] = region[a].astype(F32)
    for w in range(4):
        half_lat, half_lon = (1, 0, 1, 0)[w], (1, 1, 0, 0)[w]
        for pair in range(2):
            column = nn(pick_rows[half_lat, pair], ids[...].astype(BF16))
            column = jnp.sum(column * pick_cols[half_lon].astype(F32), axis=-1, keepdims=True)
            square = (SPAN, SPAN)
            same = lax.broadcasted_iota(jnp.int32, square, 0) == lax.broadcasted_iota(jnp.int32, square, 1)
            spots = jnp.where(same, column, 0.0).astype(BF16)
            tag_cols[place(w, pair)] = column
            tag_rows[place(w, pair)] = nn(jnp.ones((8, SPAN), BF16), spots)

    forward(0)
    for copy in far:
        copy.wait_recv()
    begin(1)
    send_halo(0, 1)
    send_halo(2, 1)
    pass_on(0, 0)
    forward(1)

    @pl.loop(1, 4)
    def _(i):
        pass_on(0, i)

    sizes = (112, 112, 48)

    def gather_windows(pair):
        for n in range(3):
            halos[n, pair].wait_recv()
        for w in range(4):
            start, height = SLABS[w]
            total = 0.0
            for part in range(2):
                chosen = gathers[w, :, pl.ds(part * LEVEL, LEVEL)][:, start:start + height]
                total += nn(chosen, slab(pair, part, start, height))
            for k, arrived in enumerate((w_in, n_in, c_in)):
                if SIDES[w][k] is not None:
                    total += nn(
                        sides[w, :, pl.ds(k * 128, sizes[k])], arrived[pl.ds(pair * sizes[k], sizes[k]), :]
                    )
            windows[pl.ds(place(w, pair) * SPAN, SPAN), :] = total.astype(BF16)

    loads[7].wait()
    loads[8].wait()
    gather_windows(0)
    pass_on(1, 0)
    loads[9].wait()
    unpack(0)

    @pl.loop(1, 4)
    def _(i):
        pass_on(1, i)

    unpack(1)
    proj_copy = pltpu.make_async_copy(whole_proj, proj_out, out_sem.at[4])
    proj_copy.start()

    def project_in(start, count):
        rows = pl.ds(start * SPAN, count * SPAN)
        for n in range(6):
            qkv[n, rows, :] = nt(windows[rows, :], whole_qkv[pl.ds(n * 256, 256), :]).astype(BF16)

    lower = lax.broadcasted_iota(jnp.int32, (SPAN, 128), 1) < 64
    ones = jnp.ones((SPAN, 128), BF16)

    def attend(w):
        rows = pl.ds(w * SPAN if isinstance(w, int) else pl.multiple_of(w * SPAN, 16), SPAN)
        bias = jnp.where(tag_cols[w] == tag_rows[w][0:1], 0.0, -1e30)
        bias = jnp.concatenate([bias, bias], axis=0)
        scores = []
        for t in range(4):
            lanes = slice((t % 2) * 128, (t % 2) * 128 + 128)
            query = qkv[t // 2, rows, lanes]
            zero = jnp.zeros_like(query)
            both = jnp.concatenate([jnp.where(lower, query, zero), jnp.where(lower, zero, query)], axis=0)
            scores.append(nt(both, qkv[2 + t // 2, rows, lanes]) + bias)
        raised = [
            jnp.exp2((score - jnp.max(score, axis=-1, keepdims=True)) * SCALE).astype(BF16) for score in scores
        ]
        for t in range(4):
            lanes = slice((t % 2) * 128, (t % 2) * 128 + 128)
            mixed = nn(raised[t], jnp.concatenate([qkv[4 + t // 2, rows, lanes], ones], axis=1))
            top = jnp.where(lower, mixed[:SPAN, :128], mixed[SPAN:, :128])
            bottom = jnp.where(lower, mixed[:SPAN, 128:], mixed[SPAN:, 128:])
            attended[w, :, pl.ds(t * 128, 128)] = (top / bottom).astype(BF16)

    returns = {}

    def give_back(k, sources, pair, target):
        total = 0.0
        for w in sources:
            total += nn(sides_t[w, pl.ds(k * 128, sizes[k]), :], attended[place(w, pair)])
        rows = pl.ds(pair * sizes[k], sizes[k])
        src, dst = ((w_back, w_home), (n_back, n_home), (c_back, c_home))[k]
        src[rows, :] = total.astype(BF16)
        copy = remote(src.at[rows, :], dst.at[rows, :], back_send.at[k, pair], back_recv.at[k, pair], target)
        copy.start()
        returns[k, pair] = copy

    loads[10].wait()
    project_in(0, 2)

    @pl.loop(0, 2, unroll=2)
    def _(w):
        attend(w)

    give_back(0, (0, 1), 0, beside(0, 1))
    give_back(2, (0,), 0, beside(1, 1))
    gather_windows(1)
    project_in(2, 4)

    @pl.loop(2, 5, unroll=3)
    def _(w):
        attend(w)

    give_back(0, (0, 1), 1, beside(0, 1))
    give_back(2, (0,), 1, beside(1, 1))
    give_back(1, (0, 2), 0, beside(1, 0))
    attend(5)
    give_back(1, (0, 2), 1, beside(1, 0))
    project_in(6, 2)

    @pl.loop(6, 8, unroll=2)
    def _(w):
        attend(w)

    loads[11].wait()
    for pair in range(2):
        for part in range(2):
            total = 0.0
            for w in range(4):
                total += nn(gathers_t[w, pl.ds(part * LEVEL, LEVEL), :], attended[place(w, pair)])
            restored[own_level(pair, part)] = total

    loads[12].wait()
    written = [proj_copy]
    for pair in range(2):
        for k in (1, 2, 0):
            returns[k, pair].wait_recv()
        for part in range(2):
            level = own_level(pair, part)
            total = restored[level]
            for k, home in enumerate((w_home, n_home, c_home)):
                total += nn(
                    packs_t[pl.ds(part * LEVEL, LEVEL), pl.ds(k * 128, sizes[k])],
                    home[pl.ds(pair * sizes[k], sizes[k]), :],
                )
            rows = pl.ds(level * LEVEL, LEVEL)
            given[rows, :] = total.astype(BF16)
            copy = pltpu.make_async_copy(given.at[rows, :], restored_out.at[rows, :], out_sem.at[level])
            copy.start()
            written.append(copy)

    for copy in [*first, *far, *halos.values(), *returns.values()]:
        copy.wait_send()
    for part in range(2):
        for d in (1, 2, 3):
            step_one(part, d).wait_send()

        @pl.loop(0, 4)
        def _(i):
            for d in (1, 2, 3):
                step_two(part, i, d).wait_send()
            for k in range(4):
                relay(part, i, k).wait_send()

    for copy in written:
        copy.wait()


def constants():
    packs = np.concatenate(PACKS, axis=0)
    gathers = np.stack(GATHERS)
    sides = np.zeros((3, SPAN, 384), np.float32)
    for w in range(3):
        for k, matrix in enumerate(SIDES[w]):
            if matrix is not None:
                sides[w, :, k * 128:k * 128 + matrix.shape[1]] = matrix
    packs_t = np.zeros((2 * LEVEL, 384), np.float32)
    for k, matrix in enumerate(PACKS):
        packs_t[:, k * 128:k * 128 + matrix.shape[0]] = matrix.T
    pick_rows, pick_cols = tag_picks()
    return [
        jnp.asarray(a, BF16)
        for a in (
            packs, gathers, sides, lane_moves(), packs_t, gathers.transpose(0, 2, 1), sides.transpose(0, 2, 1),
            pick_rows, pick_cols,
        )
    ]


def local(tokens, region, qkv_weight, proj_weight):
    flat = tokens.reshape(-1, D)
    operands = [flat, region.transpose(1, 0, 2), qkv_weight, proj_weight.T, *constants()]
    operands = [pltpu.with_memory_space_constraint(a, pltpu.HBM) for a in operands]
    anywhere = pl.BlockSpec(memory_space=pl.ANY)
    dma = pltpu.SemaphoreType.DMA

    def pieces():
        return [pltpu.VMEM((n, D), BF16) for n in (224, 224, 96)]

    restored, whole_proj = pl.pallas_call(
        kernel,
        out_shape=[jax.ShapeDtypeStruct(flat.shape, BF16), jax.ShapeDtypeStruct((D, D), BF16)],
        in_specs=[anywhere] * len(operands),
        out_specs=[anywhere] * 2,
        scratch_shapes=[
            *[pltpu.VMEM(a.shape, a.dtype) for a in operands],
            pltpu.VMEM((ROWS * LEVELS, COLS), F32),
            pltpu.VMEM((8, 8, SPAN), F32),
            pltpu.VMEM((8, SPAN, 1), F32),
            pltpu.VMEM((LEVELS * LEVEL, D), BF16),
            pltpu.VMEM((8 * SPAN, D), BF16),
            pltpu.VMEM((6, 8 * SPAN, 256), BF16),
            pltpu.VMEM((8, SPAN, D), BF16),
            pltpu.VMEM((LEVELS, LEVEL, D), F32),
            pltpu.VMEM((LEVELS * LEVEL, D), BF16),
            pltpu.VMEM((2, 4, 4, 16, 16, 128), BF16),
            pltpu.VMEM((3 * D, D), BF16),
            pltpu.VMEM((D, D), BF16),
            *pieces(), *pieces(), *pieces(), *pieces(),
            dma((len(operands),)), dma((5,)),
            dma((10,)), dma((11,)), dma((2, 4, 4)), dma((2, 4, 4)), dma((2, 4, 4)), dma((2, 4, 4)),
            dma((3, 2)), dma((3, 2)), dma((3, 2)), dma((3, 2)),
        ],
        compiler_params=pltpu.CompilerParams(
            collective_id=0, has_side_effects=True, vmem_limit_bytes=34 * 1024 * 1024
        ),
        name="attention_block",
    )(*operands)
    blended = flat.astype(F32) + nt(restored, whole_proj)
    return blended.astype(BF16).reshape(tokens.shape)


def solution(mesh):
    placed = (P(None, "lat", "lon", None), P(None, "lat", "lon"), P("lat", "lon"), P("lat", "lon"))
    return jax.shard_map(
        local, mesh=mesh, in_specs=placed, out_specs=P(None, "lat", "lon", None), check_vma=False
    )
```
